128 devices in a mesh: section: 2 (over z_lo), seq: 8 (over y, z_hi), wa: 8 (over x, core).
Axes of the slice: x: 4, y: 4, z: 4 (z_hi: 2, z_lo: 2; z = z_hi * 2 + z_lo), core: 2. Of those that a mesh axis runs over, the one named last changes fastest.
Arguments:
- first_layer_input: bfloat16 [2, 1536, 1024], P(None, 'wa', 'seq'), may hold values from -6 to 6
- routes: int32 [2, 2, 1024, 8], P('section', None, 'seq'), may hold values from 0 to 39, all different within a row; in each aligned block of 128 rows (0 to 127, 128 to 255, ..., all dimensions but the last counted through in order) at most 32 rows name the same one
- cotangent: bfloat16 [2, 1536, 1024], P(None, 'wa', 'seq'), may hold values from -6 to 6
- gains: float32 [2, 2, 1536], P('section', None, 'wa'), may hold values from 0.1 to 1.9
- qkv_weight: bfloat16 [2, 1536, 2560], P('section', 'wa'), may hold values from -0.15625 to 0.15625
- out_weight: bfloat16 [2, 1536, 1536], P('section', 'wa'), may hold values from -0.875 to 0.875
- router_weight: bfloat16 [2, 1536, 40], P('section', 'wa'), may hold values from -0.078125 to 0.078125
- expert_in: bfloat16 [2, 40, 2, 512, 1536], P('section', None, None, 'wa'), may hold values from -0.15625 to 0.15625
- expert_out: bfloat16 [2, 40, 512, 1536], P('section', None, 'wa'), may hold values from -0.25 to 0.25
Outputs:
- layer_outputs: bfloat16 [2, 2, 1024, 1536], P('section', None, 'seq', 'wa')
- input_grads: float32 [2, 2, 1024, 1536], P('section', None, 'seq', 'wa')
- gain_grads: float32 [2, 2, 1536], P('section', None, 'wa')
- qkv_grads: float32 [2, 1536, 2560], P('section', 'wa', 'seq')
- attn_out_grads: float32 [2, 1536, 1536], P('section', 'wa', 'seq')
- router_grads: float32 [2, 1536, 40], P('section', 'wa')
- expert_in_grads: float32 [2, 40, 2, 512, 1536], P('section', None, None, 'wa', 'seq')
- expert_out_grads: float32 [2, 40, 512, 1536], P('section', None, 'wa', 'seq')
The draws below stay inside these ranges and needn't reach their ends.
Inputs may be any that keep to these rules, and one draw needn't show every extreme that they name: `routes`: in each aligned block of 128 rows (the rows of one device along seq) no expert is named by more than 32 rows, a bound that some block reaches; the 8 experts of a row differ.
All inputs are finite; a program needn't handle non-finite values.
Results may differ from the reference program's by a relative error of at most 0.04.
Values may be sent and summed in bfloat16 or wider, within the bound.
No kernel may reach another device: no remote copies, remote signals or barrier semaphores. Data moves between devices by JAX's collectives and lax.ppermute only.
A program may use at most 320 MiB of HBM per device.

```python
import math
import jax
import jax.numpy as jnp
import numpy as np
from jax import lax

D = 1536
HEADS = 24
KV_HEADS = 8
HEAD_DIM = 64
EXPERTS = 40
EXPERT_FF = 512
TOP = 8
MICRO = 2
LAYERS = 2
SEQ_LEN = 1024
ROWS = 128
CAP = 32
Q_COLS = 1536
QKV_COLS = 2560
N_SEQ = 8


def shard_levels(rng, extent, shards, smallest, largest):
    factor_of = 1.0
    for position, shards_of in shards:
        steps = jax.random.uniform(jax.random.fold_in(jax.random.fold_in(rng, 6), position), (shards_of,), jnp.float32, smallest / len(shards), largest / len(shards))
        factor_of = factor_of * jnp.repeat(jnp.exp(steps), extent[position] // shards_of).reshape((-1,) + (1,) * (len(extent) - 1 - position))
    return factor_of


def shared_out(own_key, own, number, rows, count, top, most, skew):
    sequence = jax.random.permutation(own_key, count)
    crowded, ordinary = portions_of(count, rows * top, most, skew, True), portions_of(count, rows * top, most, skew, False)
    places = jnp.arange(count)

    def named(tallies, rotation):
        used = int((tallies > 0).sum())
        fixed = max(1, used // 4)
        moved = fixed + (places - fixed + rotation * (used - fixed)) % max(1, count - fixed)
        return jnp.zeros((count,), jnp.int32).at[sequence[jnp.where(places < fixed, places, moved)]].set(jnp.asarray(tallies, jnp.int32))

    tallies = jnp.where(number % 4 == 0, named(crowded, number // 4), named(ordinary, number - number // 4 - 1))
    mixed = jax.random.permutation(jax.random.fold_in(own, 3), count)
    donor, receiver = mixed[0:count // 2 * 2:2], mixed[1:count // 2 * 2:2]
    room = jnp.minimum(tallies[donor] - 1, most - tallies[receiver]) // 2
    room = jnp.where((donor == sequence[0]) | (receiver == sequence[0]) | (tallies[receiver] == 0), 0, jnp.maximum(room, 0))
    moved = jax.random.randint(jax.random.fold_in(own, 4), (count // 2,), 0, 1 << 20) % (room + 1)
    tallies = tallies.at[donor].add(-moved).at[receiver].add(moved)
    members = jnp.searchsorted(jnp.cumsum(tallies), jnp.arange(rows * top), side="right").astype(jnp.int32)
    listing = members.reshape(top, rows).T
    listing = listing[jax.random.permutation(jax.random.fold_in(own, 1), rows)]
    rotation = jax.random.randint(jax.random.fold_in(own, 2), (rows, 1), 0, top)
    return jnp.take_along_axis(listing, (jnp.arange(top)[None, :] + rotation) % top, axis=1)


def portions_of(number_of, total, most, lean, full):
    weights = [(1 << 20) // math.isqrt(rank ** lean) + 1 for rank in range(1, number_of + 1)]
    largest = most if full else min(most, max(-(-total // number_of), total * weights[0] // sum(weights)))
    least = 1 if total - largest >= number_of - 1 else 0
    holding, surplus = [largest] + [least] * (number_of - 1), total - largest - least * (number_of - 1)
    while surplus > 0:
        candidates = [i for i in range(1, number_of) if holding[i] < largest] or [i for i in range(1, number_of) if holding[i] < most]
        pool, remaining = sum([weights[i] for i in candidates]), surplus
        for i in candidates:
            addition = min(most - holding[i], max(1, remaining * weights[i] // pool), surplus)
            holding[i] = holding[i] + addition
            surplus = surplus - addition
    return np.array(holding)


def noise(rng, extent, scale, bound, cuts=(), held_as=jnp.bfloat16):
    entries = jax.random.normal(rng, extent, jnp.float32) * scale
    if len(cuts) > 0:
        entries = shard_levels(rng, extent, cuts, -0.22, 0.18) * entries
    return jnp.clip(entries, min=-bound, max=bound).astype(held_as)


def setup_inputs(seed: int = 0) -> dict:
    key_of = jax.random.split(jax.random.key(seed), 10)
    first_layer_input = noise(key_of[0], (MICRO, D, SEQ_LEN), 1.0, 6.0, ((1, 8), (2, 8)))
    routes_keys = jax.random.split(jax.random.fold_in(key_of[1], 1), LAYERS * MICRO * SEQ_LEN // ROWS)
    routes_turns = jax.random.permutation(jax.random.fold_in(key_of[1], 3), LAYERS * MICRO * SEQ_LEN // ROWS)
    routes = jax.vmap(lambda own, number: shared_out(jax.random.fold_in(key_of[1], 2), own, number, ROWS, EXPERTS, TOP, CAP, 1))(routes_keys, routes_turns).reshape((LAYERS, MICRO, SEQ_LEN, TOP))
    cotangent = noise(key_of[2], (MICRO, D, SEQ_LEN), 1.0, 6.0, ((1, 8), (2, 8)))
    gains = jnp.clip(1.0 + 0.18 * jax.random.normal(key_of[3], (LAYERS, 2, D), jnp.float32), 0.1, 1.9)
    qkv_weight = noise(key_of[4], (LAYERS, D, QKV_COLS), D ** -0.5, 0.15625, ((0, 2), (1, 8)))
    out_weight = noise(key_of[5], (LAYERS, D, Q_COLS), (Q_COLS // 32) ** -0.5, 0.875, ((0, 2), (1, 8)))
    router_weight = noise(key_of[6], (LAYERS, D, EXPERTS), (4 * D) ** -0.5, 0.078125, ((0, 2), (1, 8)))
    expert_in = noise(key_of[7], (LAYERS, EXPERTS, 2, EXPERT_FF, D), D ** -0.5, 0.15625, ((0, 2), (3, 8)))
    expert_out = noise(key_of[8], (LAYERS, EXPERTS, EXPERT_FF, D), EXPERT_FF ** -0.5, 0.25, ((0, 2), (2, 8)))
    return dict(first_layer_input=first_layer_input, routes=routes, cotangent=cotangent, gains=gains, qkv_weight=qkv_weight, out_weight=out_weight, router_weight=router_weight, expert_in=expert_in, expert_out=expert_out)


@jax.custom_vjp
def low(v):
    return lax.optimization_barrier(v.astype(jnp.bfloat16)).astype(jnp.float32)

@jax.custom_vjp
def low_back(v):
    return v

def low_keep(v):
    return (low(v), None)

def low_pass(kept, grad):
    return (grad,)

def back_keep(v):
    return (v, None)

def back_low(kept, grad):
    return (low(grad),)
low.defvjp(low_keep, low_pass)
low_back.defvjp(back_keep, back_low)
epsilon = 1e-06

def product(left, right):
    return jnp.dot(left, right, precision=lax.Precision.HIGHEST)

def batched(form, left, right):
    return jnp.einsum(form, left, right, precision=lax.Precision.HIGHEST)

def rms_norm(values, gain):
    return values * lax.rsqrt(lax.optimization_barrier(jnp.mean(values * values, axis=-1, keepdims=True)) + epsilon) * gain

def rotary_angles(positions, head_dim):
    half_dim = head_dim // 2
    frequency = 10000.0 ** (-jnp.arange(half_dim).astype(jnp.float32) * (2.0 / head_dim))
    angles = positions.astype(jnp.float32)[:, None] * frequency[None, :]
    return (jnp.cos(angles), jnp.sin(angles))

def rotate(values, cosine, sine):
    half_dim = values.shape[-1] // 2
    first_half = values[..., :half_dim]
    second_half = values[..., half_dim:]
    cosine = cosine[:, None, :]
    sine = sine[:, None, :]
    return jnp.concatenate([first_half * cosine - second_half * sine, second_half * cosine + first_half * sine], axis=-1)

def slot_table(route_ids, capacity):
    count_rows, count_top = route_ids.shape
    flat_ids = route_ids.reshape(-1).astype(jnp.int32)
    one_hot = (flat_ids[:, None] == jnp.arange(EXPERTS, dtype=jnp.int32)[None, :]).astype(jnp.int32)
    before = (jnp.cumsum(one_hot, axis=0) - one_hot).astype(jnp.int32)
    places = lax.optimization_barrier(jnp.sum(before * one_hot, axis=1)).astype(jnp.int32)
    slots = (flat_ids * capacity + places).astype(jnp.int32)
    sources = (jnp.arange(count_rows * count_top, dtype=jnp.int32) // count_top).astype(jnp.int32)
    owner = jnp.full((EXPERTS * capacity,), count_rows, jnp.int32).at[slots].set(sources)
    return (slots, owner)

def layer(resid, route_ids, gain_pair, w_qkv, w_attn, w_router, w_inner, w_outer):
    length = resid.shape[0]
    per_group = HEADS // KV_HEADS
    normed_one = low(rms_norm(resid, gain_pair[0]))
    grouped = low_back(product(normed_one, w_qkv)).reshape(length, KV_HEADS, per_group + 2, HEAD_DIM)
    cosine, sine = rotary_angles(jnp.arange(length, dtype=jnp.int32), HEAD_DIM)
    turned = rotate(grouped[:, :, :per_group + 1].reshape(length, -1, HEAD_DIM), cosine, sine)
    turned = low(jnp.concatenate([turned.reshape(length, KV_HEADS, per_group + 1, HEAD_DIM), grouped[:, :, per_group + 1:]], axis=2))
    queries = turned[:, :, :per_group]
    keys = turned[:, :, per_group]
    values = turned[:, :, per_group + 1]
    block = min(512, length)
    key_pos = jnp.arange(length, dtype=jnp.int32)

    def attend(start):
        query_block = lax.dynamic_slice_in_dim(queries, start, block, 0)
        scores = low_back(batched('bgqd,kgd->gqbk', query_block, keys) * HEAD_DIM ** (-0.5))
        query_pos = start + jnp.arange(block, dtype=jnp.int32)
        scores = jnp.where((key_pos[None, :] <= query_pos[:, None])[None, None], scores, -1e+30)
        raised = jnp.exp(scores - lax.optimization_barrier(jnp.max(scores, axis=3, keepdims=True)))
        probs = low(raised / lax.optimization_barrier(jnp.sum(raised, axis=3, keepdims=True)))
        return batched('gqbk,kgd->bgqd', probs, values).reshape(block, -1)
    starts = jnp.arange(0, length, block, dtype=jnp.int32)
    mixed = lax.map(jax.checkpoint(attend), starts).reshape(length, -1)
    mixed = low_back(low(mixed))
    middle = resid + low_back(product(mixed, w_attn.T))
    normed_two = low(rms_norm(middle, gain_pair[1]))
    logits = product(normed_two, w_router)
    gates = jax.nn.softmax(jnp.take_along_axis(logits, route_ids, axis=1), axis=1)
    inner = w_inner.reshape(EXPERTS, 2 * EXPERT_FF, D)

    def experts(pieces):
        normed_block, block_ids, block_gates = pieces
        slots, owner = slot_table(block_ids, CAP)
        padded = jnp.concatenate([normed_block, jnp.zeros((1, D), normed_block.dtype)], axis=0)
        expert_rows = padded[owner].reshape(EXPERTS, CAP, D)
        gate_up = low_back(batched('ecd,ehd->ech', expert_rows, inner))
        active = low(jax.nn.silu(gate_up[..., :EXPERT_FF]) * gate_up[..., EXPERT_FF:])
        results = low_back(batched('ech,ehd->ecd', active, w_outer)).reshape(EXPERTS * CAP, D)
        picked = results[slots].reshape(ROWS, TOP, D)
        return lax.optimization_barrier(jnp.sum(block_gates[:, :, None] * picked, axis=1))
    mixture = lax.map(jax.checkpoint(experts), (normed_two.reshape(N_SEQ, ROWS, D), route_ids.reshape(N_SEQ, ROWS, TOP), gates.reshape(N_SEQ, ROWS, TOP)))
    return middle + low_back(mixture.reshape(length, D))

def layer_params(params, index):
    return tuple((weight[index] for weight in params))

def reference(first_layer_input, routes, cotangent, gains, qkv_weight, out_weight, router_weight, expert_in, expert_out):
    params = (gains.astype(jnp.float32), qkv_weight.astype(jnp.float32), out_weight.astype(jnp.float32), router_weight.astype(jnp.float32), expert_in.astype(jnp.float32), expert_out.astype(jnp.float32))
    input_list = jnp.transpose(first_layer_input.astype(jnp.float32), (0, 2, 1))
    taps = jnp.zeros(input_list.shape, jnp.float32)

    def whole(input_list, taps, params):

        def one_micro(carry, pieces):
            x_one, first_ids, second_ids, tap_one = pieces
            first = layer(x_one, first_ids, *layer_params(params, 0))
            second = layer(low_back(low(first)) + tap_one, second_ids, *layer_params(params, 1))
            return (carry, (first, second))
        final_carry, outputs = lax.scan(one_micro, jnp.zeros((), jnp.float32), (input_list, routes[0], routes[1], taps))
        return outputs
    primal, pullback = jax.vjp(whole, input_list, taps, params)
    first_all, second_all = primal
    input_grad, tap_grad, param_grads = pullback((jnp.zeros_like(first_all), jnp.transpose(cotangent.astype(jnp.float32), (0, 2, 1))))
    layer_outputs = jnp.stack([first_all, second_all]).astype(jnp.bfloat16)
    input_grads = jnp.stack([input_grad, tap_grad])
    return (layer_outputs, input_grads, param_grads[0], param_grads[1], param_grads[2], param_grads[3], param_grads[4], param_grads[5])
```

```python
import jax
import jax.numpy as jnp
from jax import lax
from jax.experimental import pallas as pl
from jax.experimental.pallas import tpu as pltpu
from jax.sharding import PartitionSpec as P

HEADS = 24
KV_HEADS = 8
PER_GROUP = HEADS // KV_HEADS
HEAD_DIM = 64
EXPERTS = 40
TOP = 8
MICRO = 2
CAP = 32
N_SEQ = 8
N_WA = 8
ROWS = 128
WIDTH = 1536
OWN = WIDTH // N_WA
TOKENS = MICRO * ROWS
LENGTH = ROWS * N_SEQ
HIDDEN = 64
SLOTS = MICRO * CAP
GROUP_COLS = (PER_GROUP + 2) * HEAD_DIM
BATCH = 4
STEPS = EXPERTS // BATCH
BLOCK = BATCH * HIDDEN
SCALE = HEAD_DIM ** (-0.5)
EPSILON = 1e-06
BF16 = jnp.bfloat16
F32 = jnp.float32
VMEM_LIMIT = 56 * 1024 * 1024


def dot_nn(a, b):
    return lax.dot_general(a, b, (((1,), (0,)), ((), ())), preferred_element_type=F32)


def dot_nt(a, b):
    return lax.dot_general(a, b, (((1,), (1,)), ((), ())), preferred_element_type=F32)


def dot_tn(a, b):
    return lax.dot_general(a, b, (((0,), (0,)), ((), ())), preferred_element_type=F32)


def params():
    return pltpu.CompilerParams(
        vmem_limit_bytes=VMEM_LIMIT, dimension_semantics=("arbitrary",)
    )


def one_hot_slots(places):
    slot = lax.broadcasted_iota(jnp.int32, (BATCH, SLOTS, TOKENS), 1).astype(F32)
    hit = jnp.where(slot == places, 1.0, 0.0)
    return hit.reshape(BATCH * SLOTS, TOKENS).astype(BF16)


def own_slots(rows, pick, height):
    every = dot_nt(rows, pick)
    lane = lax.broadcasted_iota(jnp.int32, (height, BATCH * SLOTS), 1) // SLOTS
    out = every[:height]
    for e in range(1, BATCH):
        out = jnp.where(lane == e, every[e * height : (e + 1) * height], out)
    return out.astype(BF16)


def spread_slots(compact):
    lane = lax.broadcasted_iota(jnp.int32, compact.shape, 1) // SLOTS
    zero = jnp.zeros_like(compact)
    return jnp.concatenate([jnp.where(lane == e, compact, zero) for e in range(BATCH)], axis=0)


def experts_forward_kernel(
    x_ref, gate_ref, place_ref, win_ref, wout_ref, y_ref, g_ref, u_ref, f_ref, total
):
    step = pl.program_id(0)
    x = x_ref[...]
    wg = win_ref[:, 0].reshape(BLOCK, WIDTH)
    wu = win_ref[:, 1].reshape(BLOCK, WIDTH)
    g = dot_nn(wg, x)
    u = dot_nn(wu, x)
    g_ref[...] = g.astype(BF16)
    u_ref[...] = u.astype(BF16)
    active = (g * jax.nn.sigmoid(g) * u).astype(BF16).astype(F32)
    gated = (active.reshape(BATCH, HIDDEN, TOKENS) * gate_ref[...]).astype(BF16)
    gated = gated.reshape(BLOCK, TOKENS)
    f_ref[...] = own_slots(gated, one_hot_slots(place_ref[...]), HIDDEN)
    part = dot_tn(gated, wout_ref[...].reshape(BLOCK, WIDTH))

    @pl.when(step == 0)
    def _():
        total[...] = part

    @pl.when(step > 0)
    def _():
        total[...] += part

    @pl.when(step == STEPS - 1)
    def _():
        y_ref[...] = total[...].astype(BF16).T


def experts_forward(x, gates, places, w_in, w_out):
    return pl.pallas_call(
        experts_forward_kernel,
        grid=(STEPS,),
        in_specs=[
            pl.BlockSpec((WIDTH, TOKENS), lambda i: (0, 0)),
            pl.BlockSpec((BATCH, 1, TOKENS), lambda i: (i, 0, 0)),
            pl.BlockSpec((BATCH, 1, TOKENS), lambda i: (i, 0, 0)),
            pl.BlockSpec((BATCH, 2, HIDDEN, WIDTH), lambda i: (i, 0, 0, 0)),
            pl.BlockSpec((BATCH, HIDDEN, WIDTH), lambda i: (i, 0, 0)),
        ],
        out_specs=[
            pl.BlockSpec((WIDTH, TOKENS), lambda i: (0, 0)),
            pl.BlockSpec((BLOCK, TOKENS), lambda i: (i, 0)),
            pl.BlockSpec((BLOCK, TOKENS), lambda i: (i, 0)),
            pl.BlockSpec((HIDDEN, BATCH * SLOTS), lambda i: (0, i)),
        ],
        out_shape=[
            jax.ShapeDtypeStruct((WIDTH, TOKENS), BF16),
            jax.ShapeDtypeStruct((EXPERTS * HIDDEN, TOKENS), BF16),
            jax.ShapeDtypeStruct((EXPERTS * HIDDEN, TOKENS), BF16),
            jax.ShapeDtypeStruct((HIDDEN, EXPERTS * SLOTS), BF16),
        ],
        scratch_shapes=[pltpu.VMEM((TOKENS, WIDTH), F32)],
        compiler_params=params(),
        cost_estimate=pl.CostEstimate(
            flops=6 * TOKENS * EXPERTS * HIDDEN * WIDTH, bytes_accessed=28_000_000, transcendentals=0
        ),
        name="experts_forward",
    )(x, gates, places, w_in, w_out)


def experts_backward_kernel(
    dz_ref, g_ref, u_ref, gate_ref, place_ref, win_ref, wout_ref, dx_ref, dgate_ref, du_ref, total
):
    step = pl.program_id(0)
    through = dot_nn(wout_ref[...].reshape(BLOCK, WIDTH), dz_ref[...])
    g = g_ref[...].astype(F32)
    u = u_ref[...].astype(F32)
    sig = jax.nn.sigmoid(g)
    silu = g * sig
    active = (silu * u).astype(BF16).astype(F32)
    dgate_ref[...] = jnp.sum(
        (active * through).reshape(BATCH, HIDDEN, TOKENS), axis=1, keepdims=True
    )
    df = (through.reshape(BATCH, HIDDEN, TOKENS) * gate_ref[...]).reshape(BLOCK, TOKENS)
    dg = (df * u * (sig * (1.0 + g * (1.0 - sig)))).astype(BF16)
    du = (df * silu).astype(BF16)
    pick = one_hot_slots(place_ref[...])
    du_ref[:HIDDEN] = own_slots(dg, pick, HIDDEN)
    du_ref[HIDDEN:] = own_slots(du, pick, HIDDEN)
    part = dot_tn(dg, win_ref[:, 0].reshape(BLOCK, WIDTH))
    part += dot_tn(du, win_ref[:, 1].reshape(BLOCK, WIDTH))

    @pl.when(step == 0)
    def _():
        total[...] = part

    @pl.when(step > 0)
    def _():
        total[...] += part

    @pl.when(step == STEPS - 1)
    def _():
        dx_ref[...] = total[...].astype(BF16).T


def experts_backward(dz, g, u, gates, places, w_in, w_out):
    return pl.pallas_call(
        experts_backward_kernel,
        grid=(STEPS,),
        in_specs=[
            pl.BlockSpec((WIDTH, TOKENS), lambda i: (0, 0)),
            pl.BlockSpec((BLOCK, TOKENS), lambda i: (i, 0)),
            pl.BlockSpec((BLOCK, TOKENS), lambda i: (i, 0)),
            pl.BlockSpec((BATCH, 1, TOKENS), lambda i: (i, 0, 0)),
            pl.BlockSpec((BATCH, 1, TOKENS), lambda i: (i, 0, 0)),
            pl.BlockSpec((BATCH, 2, HIDDEN, WIDTH), lambda i: (i, 0, 0, 0)),
            pl.BlockSpec((BATCH, HIDDEN, WIDTH), lambda i: (i, 0, 0)),
        ],
        out_specs=[
            pl.BlockSpec((WIDTH, TOKENS), lambda i: (0, 0)),
            pl.BlockSpec((BATCH, 1, TOKENS), lambda i: (i, 0, 0)),
            pl.BlockSpec((2 * HIDDEN, BATCH * SLOTS), lambda i: (0, i)),
        ],
        out_shape=[
            jax.ShapeDtypeStruct((WIDTH, TOKENS), BF16),
            jax.ShapeDtypeStruct((EXPERTS, 1, TOKENS), F32),
            jax.ShapeDtypeStruct((2 * HIDDEN, EXPERTS * SLOTS), BF16),
        ],
        scratch_shapes=[pltpu.VMEM((TOKENS, WIDTH), F32)],
        compiler_params=params(),
        cost_estimate=pl.CostEstimate(
            flops=6 * TOKENS * EXPERTS * HIDDEN * WIDTH, bytes_accessed=28_000_000, transcendentals=0
        ),
        name="experts_backward",
    )(dz, g, u, gates, places, w_in, w_out)


def weight_grad_kernel(compact_ref, feature_ref, place_ref, out_ref):
    height = compact_ref.shape[1]
    total = jnp.zeros((BATCH * height, OWN), F32)
    for s in range(N_SEQ):
        pick = one_hot_slots(place_ref[s])
        rows = dot_nt(feature_ref[s], pick).astype(BF16)
        total += dot_nt(spread_slots(compact_ref[s]), rows)
    out_ref[...] = total.reshape(BATCH, height, OWN)


def weight_grad(compact, feature, places):
    height = compact.shape[1]
    return pl.pallas_call(
        weight_grad_kernel,
        grid=(STEPS,),
        in_specs=[
            pl.BlockSpec((N_SEQ, height, BATCH * SLOTS), lambda i: (0, 0, i)),
            pl.BlockSpec((N_SEQ, OWN, TOKENS), lambda i: (0, 0, 0)),
            pl.BlockSpec((N_SEQ, BATCH, 1, TOKENS), lambda i: (0, i, 0, 0)),
        ],
        out_specs=pl.BlockSpec((BATCH, height, OWN), lambda i: (i, 0, 0)),
        out_shape=jax.ShapeDtypeStruct((EXPERTS, height, OWN), F32),
        compiler_params=params(),
        cost_estimate=pl.CostEstimate(
            flops=4 * N_SEQ * TOKENS * EXPERTS * height * OWN, bytes_accessed=15_000_000, transcendentals=0
        ),
        name="expert_weight_grad",
    )(compact, feature, places)


def causal_mask(first):
    key = lax.broadcasted_iota(jnp.int32, (LENGTH, ROWS), 0)
    query = lax.broadcasted_iota(jnp.int32, (LENGTH, ROWS), 1) + first
    return key <= query


def side_by_side(parts):
    return jnp.concatenate(parts, axis=1)


def attention_forward_kernel(first_ref, q_ref, kv_ref, o_ref, lse_ref):
    keys = side_by_side([kv_ref[s, :HEAD_DIM] for s in range(N_SEQ)])
    values = side_by_side([kv_ref[s, HEAD_DIM:] for s in range(N_SEQ)])
    keep = causal_mask(first_ref[0])
    for h in range(PER_GROUP):
        rows = slice(h * HEAD_DIM, (h + 1) * HEAD_DIM)
        scores = jnp.where(keep, dot_tn(keys, q_ref[rows]) * SCALE, -1e30)
        top = jnp.max(scores, axis=0, keepdims=True)
        raised = jnp.exp(scores - top)
        total = jnp.sum(raised, axis=0, keepdims=True)
        probs = (raised * (1.0 / total)).astype(BF16)
        o_ref[rows] = dot_nn(values, probs).astype(BF16)
        lse_ref[h] = top + jnp.log(total)


def attention_forward(first, q, kv):
    return pl.pallas_call(
        attention_forward_kernel,
        grid=(MICRO,),
        in_specs=[
            pl.BlockSpec(memory_space=pltpu.SMEM),
            pl.BlockSpec((PER_GROUP * HEAD_DIM, ROWS), lambda m: (0, m)),
            pl.BlockSpec((N_SEQ, 2 * HEAD_DIM, ROWS), lambda m: (0, 0, m)),
        ],
        out_specs=[
            pl.BlockSpec((PER_GROUP * HEAD_DIM, ROWS), lambda m: (0, m)),
            pl.BlockSpec((PER_GROUP, 1, ROWS), lambda m: (0, 0, m)),
        ],
        out_shape=[
            jax.ShapeDtypeStruct((PER_GROUP * HEAD_DIM, TOKENS), BF16),
            jax.ShapeDtypeStruct((PER_GROUP, 1, TOKENS), F32),
        ],
        compiler_params=params(),
        name="attention_forward",
    )(first, q, kv)


def attention_backward_kernel(first_ref, q_ref, kv_ref, o_ref, do_ref, lse_ref, dq_ref, dkv_ref):
    keys = side_by_side([kv_ref[s, :HEAD_DIM] for s in range(N_SEQ)])
    values = side_by_side([kv_ref[s, HEAD_DIM:] for s in range(N_SEQ)])
    keep = causal_mask(first_ref[0])
    dkeys = jnp.zeros((HEAD_DIM, LENGTH), F32)
    dvalues = jnp.zeros((HEAD_DIM, LENGTH), F32)
    for h in range(PER_GROUP):
        rows = slice(h * HEAD_DIM, (h + 1) * HEAD_DIM)
        query = q_ref[rows]
        dout = do_ref[rows]
        scores = jnp.where(keep, dot_tn(keys, query) * SCALE, -1e30)
        probs = jnp.exp(scores - lse_ref[h])
        dvalues += dot_nt(dout, probs.astype(BF16))
        inner = jnp.sum(
            dout.astype(F32) * o_ref[rows].astype(F32), axis=0, keepdims=True
        )
        dscores = (probs * (dot_tn(values, dout) - inner)).astype(BF16)
        dkeys += dot_nt(query, dscores)
        dq_ref[rows] = dot_nn(keys, dscores) * SCALE
    dkeys = (dkeys * SCALE).astype(BF16)
    dvalues = dvalues.astype(BF16)
    for s in range(N_SEQ):
        lanes = slice(s * ROWS, (s + 1) * ROWS)
        dkv_ref[s, :HEAD_DIM] = dkeys[:, lanes]
        dkv_ref[s, HEAD_DIM:] = dvalues[:, lanes]


def attention_backward(first, q, kv, o, do, lse):
    q_spec = pl.BlockSpec((PER_GROUP * HEAD_DIM, ROWS), lambda m: (0, m))
    kv_spec = pl.BlockSpec((N_SEQ, 2 * HEAD_DIM, ROWS), lambda m: (0, 0, m))
    return pl.pallas_call(
        attention_backward_kernel,
        grid=(MICRO,),
        in_specs=[
            pl.BlockSpec(memory_space=pltpu.SMEM),
            q_spec,
            kv_spec,
            q_spec,
            q_spec,
            pl.BlockSpec((PER_GROUP, 1, ROWS), lambda m: (0, 0, m)),
        ],
        out_specs=[q_spec, kv_spec],
        out_shape=[
            jax.ShapeDtypeStruct((PER_GROUP * HEAD_DIM, TOKENS), F32),
            jax.ShapeDtypeStruct((N_SEQ, 2 * HEAD_DIM, TOKENS), BF16),
        ],
        compiler_params=params(),
        name="attention_backward",
    )(first, q, kv, o, do, lse)


def rotate(values, cosine, sine):
    half = HEAD_DIM // 2
    a, b = values[:, :half], values[:, half:]
    return jnp.concatenate([a * cosine - b * sine, b * cosine + a * sine], axis=1)


def high_low(values):
    high = values.astype(BF16)
    return high, (values - high.astype(F32)).astype(BF16)


def exchange(blocks, axis):
    return lax.all_to_all(blocks, axis, split_axis=0, concat_axis=0, tiled=False)


def summed(blocks, axis):
    return jnp.sum(exchange(blocks, axis).astype(F32), axis=0)


def on_device(
    first_layer_input,
    routes,
    cotangent,
    gains,
    qkv_weight,
    out_weight,
    router_weight,
    expert_in,
    expert_out,
):
    section_first = lax.axis_index("section") == 0
    s_index = lax.axis_index("seq")
    w_index = lax.axis_index("wa")
    first = jnp.reshape(s_index * ROWS, (1,)).astype(jnp.int32)

    def rows_of(values):
        return lax.all_gather(values, "wa", axis=0, tiled=True)

    def own(values):
        return lax.dynamic_slice_in_dim(values, w_index * OWN, OWN, 0)

    def lanes(values):
        return jnp.concatenate([values[0], values[1]], axis=1)

    def of_section(one, two):
        return jnp.where(section_first, one, two)

    x_first = lanes(first_layer_input)
    cot = lanes(cotangent)
    x_first_full = rows_of(x_first)
    w_qkv = qkv_weight[0]
    w_qkv_group = exchange(
        jnp.transpose(w_qkv.reshape(OWN, KV_HEADS, GROUP_COLS), (1, 0, 2)), "wa"
    ).reshape(WIDTH, GROUP_COLS)
    small = rows_of(jnp.concatenate([gains[0].T, router_weight[0].astype(F32)], axis=1))
    gain_one, gain_two = small[:, 0:1], small[:, 1:2]
    w_router = small[:, 2:].astype(BF16)
    w_attn_full = rows_of(out_weight[0])
    w_attn_group = lax.dynamic_slice_in_dim(w_attn_full, w_index * OWN, OWN, 1)
    cot_full = rows_of(cot)
    w_in = expert_in[0]
    w_out = expert_out[0]
    own_gain_one = gains[0, 0][:, None]
    own_gain_two = gains[0, 1][:, None]

    position = (s_index * ROWS + jnp.arange(ROWS, dtype=jnp.int32)).astype(F32)
    frequency = 10000.0 ** (
        -jnp.arange(HEAD_DIM // 2).astype(F32) * (2.0 / HEAD_DIM)
    )
    angle = frequency[:, None] * position[None, :]
    cosine = jnp.tile(jnp.cos(angle), (1, MICRO))
    sine = jnp.tile(jnp.sin(angle), (1, MICRO))

    experts = jnp.arange(EXPERTS, dtype=jnp.int32)[None, :, None]
    chosen = jnp.zeros((MICRO, EXPERTS, ROWS), F32)
    for k in range(TOP):
        chosen += (routes[0][:, None, :, k] == experts).astype(F32)
    earlier = jnp.triu(jnp.ones((ROWS, ROWS), BF16), 1)
    rank = jnp.einsum("met,tu->meu", chosen.astype(BF16), earlier, preferred_element_type=F32)
    micro = jnp.arange(MICRO, dtype=jnp.int32).astype(F32)[:, None, None]
    place = lanes(jnp.where(chosen > 0.5, rank + CAP * micro, -1.0))
    chosen = lanes(chosen) > 0.5
    places_all = lax.all_gather(place.astype(BF16), "seq", axis=0, tiled=False)
    places_all = places_all.astype(F32)[:, :, None, :]
    places = place[:, None, :]
    route_lanes = jnp.concatenate([routes[0, 0].T, routes[0, 1].T], axis=1)
    picked = (
        route_lanes[:, None, :] == jnp.arange(EXPERTS, dtype=jnp.int32)[None, :, None]
    )

    def norm_scale(values):
        return lax.rsqrt(jnp.mean(values * values, axis=0, keepdims=True) + EPSILON)

    def forward(x_own, x_full):
        x = x_full.astype(F32)
        scale_one = norm_scale(x)
        normed_one = (x * scale_one * gain_one).astype(BF16)
        heads = dot_tn(w_qkv_group, normed_one).reshape(PER_GROUP + 2, HEAD_DIM, TOKENS)
        turned = rotate(heads[: PER_GROUP + 1], cosine, sine)
        turned = jnp.concatenate([turned, heads[PER_GROUP + 1 :]], axis=0).astype(BF16)
        turned = turned.reshape(GROUP_COLS, TOKENS)
        queries = turned[: PER_GROUP * HEAD_DIM]
        key_value = exchange(
            jnp.broadcast_to(
                turned[PER_GROUP * HEAD_DIM :][None], (N_SEQ, 2 * HEAD_DIM, TOKENS)
            ),
            "seq",
        )
        mixed, log_total = attention_forward(first, queries, key_value)
        mixed_full = rows_of(mixed)
        middle = x + dot_nn(w_attn_full, mixed_full)
        scale_two = norm_scale(middle)
        normed_two = (middle * scale_two * gain_two).astype(BF16)
        logits = dot_tn(w_router, normed_two)
        raised = jnp.where(
            chosen,
            jnp.exp(logits - jnp.max(jnp.where(chosen, logits, -1e30), axis=0, keepdims=True)),
            0.0,
        )
        gates = raised / jnp.sum(raised, axis=0, keepdims=True)
        part, g, u, compact = experts_forward(
            normed_two, gates[:, None, :], places, w_in, w_out
        )
        out = own(middle) + summed(part.reshape(N_WA, OWN, TOKENS), "wa")
        saved = (
            x_own,
            scale_one,
            own(normed_one),
            queries,
            key_value,
            log_total,
            mixed,
            mixed_full,
            middle,
            scale_two,
            normed_two,
            logits,
            gates,
            g,
            u,
        )
        return out.astype(BF16), compact, saved

    def backward(dz, dz_full, saved):
        (
            x_own,
            scale_one,
            own_normed_one,
            queries,
            key_value,
            log_total,
            mixed,
            mixed_full,
            middle,
            scale_two,
            normed_two,
            logits,
            gates,
            g,
            u,
        ) = saved
        part, dgate, du = experts_backward(
            dz_full, g, u, gates[:, None, :], places, w_in, w_out
        )
        inner = jnp.sum(part.astype(F32) * middle * gain_two, axis=0, keepdims=True)
        dgate_top = jnp.sum(jnp.where(picked, dgate[:, 0][None], 0.0), axis=1)
        extra = jnp.concatenate(
            [
                dgate_top.astype(BF16),
                *high_low(inner),
                jnp.zeros((16 - TOP - 2, TOKENS), BF16),
            ],
            axis=0,
        )
        blocks = jnp.concatenate(
            [
                part.reshape(N_WA, OWN, TOKENS),
                jnp.broadcast_to(extra[None], (N_WA, 16, TOKENS)),
            ],
            axis=1,
        )
        back = summed(blocks, "wa")
        dgate_top = back[OWN : OWN + TOP]
        inner = back[OWN + TOP : OWN + TOP + 1] + back[OWN + TOP + 1 : OWN + TOP + 2]
        dgate = jnp.sum(jnp.where(picked, dgate_top[:, None, :], 0.0), axis=0)
        dlogit = gates * (dgate - jnp.sum(gates * dgate, axis=0, keepdims=True))
        dlogit_high, dlogit_low = high_low(dlogit)
        own_router = router_weight[0]
        dnormed = back[:OWN] + dot_nn(own_router, dlogit_high) + dot_nn(own_router, dlogit_low)
        inner += jnp.sum(dlogit * logits, axis=0, keepdims=True) / scale_two
        own_middle = own(middle)
        dmiddle = (
            dz.astype(F32)
            + scale_two * own_gain_two * dnormed
            - own_middle * (scale_two * scale_two * scale_two * inner * (1.0 / WIDTH))
        )
        gain_two_grad = jnp.sum(dnormed * own_middle * scale_two, axis=1, keepdims=True)
        own_normed_two = own(normed_two)
        router_grad = dot_nt(own_normed_two, dlogit_high) + dot_nt(own_normed_two, dlogit_low)
        dmiddle_low = dmiddle.astype(BF16)
        attn_grad = dot_nt(dmiddle_low, mixed_full)
        dmixed = dot_tn(w_attn_group, rows_of(dmiddle_low)).astype(BF16)
        dq, dkv = attention_backward(first, queries, key_value, mixed, dmixed, log_total)
        dkv = summed(dkv, "seq")
        dturned = jnp.concatenate([dq, dkv], axis=0)
        turned = jnp.concatenate(
            [queries, lax.dynamic_index_in_dim(key_value, s_index, 0, False)], axis=0
        )
        inner_one = jnp.sum(dturned * turned.astype(F32), axis=0, keepdims=True)
        dheads = dturned.reshape(PER_GROUP + 2, HEAD_DIM, TOKENS)
        dheads = jnp.concatenate(
            [rotate(dheads[: PER_GROUP + 1], cosine, -sine), dheads[PER_GROUP + 1 :]], axis=0
        )
        full = lax.all_gather(
            jnp.concatenate(
                [
                    dheads.reshape(GROUP_COLS, TOKENS).astype(BF16),
                    *high_low(inner_one),
                    jnp.zeros((14, TOKENS), BF16),
                ],
                axis=0,
            ),
            "wa",
            axis=0,
            tiled=False,
        )
        dheads_full = full[:, :GROUP_COLS].reshape(KV_HEADS * GROUP_COLS, TOKENS)
        inner_one = jnp.sum(
            full[:, GROUP_COLS : GROUP_COLS + 2].astype(F32), axis=(0, 1)
        )[None] / scale_one
        dnormed_one = dot_nn(w_qkv, dheads_full)
        x = x_own.astype(F32)
        dx = (
            dmiddle
            + scale_one * own_gain_one * dnormed_one
            - x * (scale_one * scale_one * scale_one * inner_one * (1.0 / WIDTH))
        )
        gain_one_grad = jnp.sum(dnormed_one * x * scale_one, axis=1, keepdims=True)
        qkv_grad = dot_nt(own_normed_one, dheads_full)
        return dx, du, gain_one_grad, gain_two_grad, router_grad, attn_grad, qkv_grad

    out_one, compact_one, saved_one = forward(x_first, x_first_full)
    received = lax.ppermute(out_one, "section", [(0, 1)])
    out_two, compact_two, saved_two = forward(received, rows_of(received))

    feature_in = exchange(
        of_section(saved_one[10], saved_two[10]).reshape(N_SEQ, OWN, TOKENS), "seq"
    )
    compact_out = lax.all_gather(of_section(compact_one, compact_two), "seq", axis=0, tiled=False)

    back_two = backward(cot, cot_full, saved_two)
    returned = lax.ppermute(back_two[0].astype(BF16), "section", [(1, 0)])
    returned_full = rows_of(returned)
    feature_out = exchange(
        of_section(returned_full, cot_full).reshape(N_SEQ, OWN, TOKENS), "seq"
    )
    expert_out_grad = weight_grad(compact_out, feature_out, places_all)
    back_one = backward(returned, returned_full, saved_one)

    compact_in = lax.all_gather(of_section(back_one[1], back_two[1]), "seq", axis=0, tiled=False)
    expert_in_grad = weight_grad(compact_in, feature_in, places_all)
    gain_one_grad, gain_two_grad, router_grad, attn_grad, qkv_grad = (
        of_section(one, two) for one, two in zip(back_one[2:], back_two[2:])
    )
    small_grad = lax.psum(jnp.concatenate([gain_two_grad, router_grad], axis=1), "seq")
    attn_grad = summed(
        jnp.transpose(attn_grad.astype(BF16).reshape(OWN, N_SEQ, OWN), (1, 0, 2)), "seq"
    )
    qkv_blocks = jnp.transpose(
        qkv_grad.astype(BF16).reshape(OWN, N_SEQ, GROUP_COLS), (1, 0, 2)
    )
    gain_blocks = jnp.concatenate(
        [*high_low(gain_one_grad), jnp.zeros((OWN, 384 - GROUP_COLS - 2), BF16)], axis=1
    )
    qkv_grad = summed(
        jnp.concatenate(
            [qkv_blocks, jnp.broadcast_to(gain_blocks[None], (N_SEQ,) + gain_blocks.shape)],
            axis=2,
        ),
        "seq",
    )
    gain_one_grad = qkv_grad[:, GROUP_COLS] + qkv_grad[:, GROUP_COLS + 1]

    def tokens_first(values):
        return jnp.transpose(values.reshape(OWN, MICRO, ROWS), (1, 2, 0))[None]

    return (
        tokens_first(of_section(out_one, out_two)),
        tokens_first(of_section(back_one[0], back_two[0])),
        jnp.stack([gain_one_grad, small_grad[:, 0]])[None],
        qkv_grad[None, :, :GROUP_COLS],
        attn_grad[None],
        small_grad[None, :, 1:],
        expert_in_grad.reshape(1, EXPERTS, 2, HIDDEN, OWN),
        expert_out_grad[None],
    )


def solution(mesh):
    return jax.shard_map(
        on_device,
        mesh=mesh,
        in_specs=(
            P(None, "wa", "seq"),
            P("section", None, "seq", None),
            P(None, "wa", "seq"),
            P("section", None, "wa"),
            P("section", "wa", None),
            P("section", "wa", None),
            P("section", "wa", None),
            P("section", None, None, "wa", None),
            P("section", None, "wa", None),
        ),
        out_specs=(
            P("section", None, "seq", "wa"),
            P("section", None, "seq", "wa"),
            P("section", None, "wa"),
            P("section", "wa", "seq"),
            P("section", "wa", "seq"),
            P("section", "wa", None),
            P("section", None, None, "wa", "seq"),
            P("section", None, "wa", "seq"),
        ),
        check_vma=False,
    )
```

```python
import jax
import jax.numpy as jnp
from jax import lax
from jax.experimental import pallas as pl
from jax.experimental.pallas import tpu as pltpu
from jax.sharding import PartitionSpec as P

HEADS = 24
KV_HEADS = 8
PER_GROUP = HEADS // KV_HEADS
HEAD_DIM = 64
EXPERTS = 40
TOP = 8
MICRO = 2
CAP = 32
N_SEQ = 8
N_WA = 8
ROWS = 128
WIDTH = 1536
OWN = WIDTH // N_WA
TOKENS = MICRO * ROWS
LENGTH = ROWS * N_SEQ
HIDDEN = 64
SLOTS = MICRO * CAP
GROUP_COLS = (PER_GROUP + 2) * HEAD_DIM
QUAD = 4
COLUMNS = 256
FORWARD_CHUNKS = (8, 16, 16)
BACKWARD_CHUNKS = (8, 16, 16)
SCALE = HEAD_DIM ** (-0.5)
EPSILON = 1e-06
BF16 = jnp.bfloat16
F32 = jnp.float32
VMEM_LIMIT = 20 * 1024 * 1024
EXPERT_VMEM = 48 * 1024 * 1024


def dot_nn(a, b):
    return lax.dot_general(a, b, (((1,), (0,)), ((), ())), preferred_element_type=F32)


def dot_nt(a, b):
    return lax.dot_general(a, b, (((1,), (1,)), ((), ())), preferred_element_type=F32)


def dot_tn(a, b):
    return lax.dot_general(a, b, (((0,), (0,)), ((), ())), preferred_element_type=F32)


def params():
    return pltpu.CompilerParams(
        vmem_limit_bytes=VMEM_LIMIT, dimension_semantics=("arbitrary",)
    )


def one_hot_slots(places):
    slot = lax.broadcasted_iota(jnp.int32, (QUAD, SLOTS, TOKENS), 1).astype(F32)
    hit = jnp.where(slot == places, 1.0, 0.0)
    return hit.reshape(QUAD * SLOTS, TOKENS).astype(BF16)


def chunk_starts(chunks):
    return [sum(chunks[:c]) for c in range(len(chunks))]


def copies_in(sources, targets, sems, order, chunks):
    copies = [[] for _ in sources]
    for c, (first, size) in enumerate(zip(chunk_starts(chunks), chunks)):
        for k in order:
            rows = sources[k].shape[0] // EXPERTS
            part = pl.ds(first * rows, size * rows)
            copy = pltpu.make_async_copy(sources[k].at[part], targets[k].at[part], sems.at[k, c])
            copy.start()
            copies[k].append(copy)
    return copies


def accumulate(first, total, left, right_ref):
    for c in range(0, WIDTH, COLUMNS):
        cols = slice(c, c + COLUMNS)
        part = dot_tn(right_ref[..., cols].reshape(left.shape[0], COLUMNS), left)
        if first:
            total[cols] = part
        else:
            total[cols] += part


def experts_forward_kernel(
    x_ref, gate_ref, place_ref, win_hbm, wout_hbm,
    y_ref, f_ref, g_hbm, u_hbm,
    win, wout, g_all, u_all, total, in_sems, out_sems,
):
    arriving = copies_in((win_hbm, wout_hbm), (win, wout), in_sems, (0, 1), FORWARD_CHUNKS)
    leaving = []
    lane = lax.broadcasted_iota(jnp.int32, (SLOTS, 2 * HIDDEN), 1)
    for c, (first, size) in enumerate(zip(chunk_starts(FORWARD_CHUNKS), FORWARD_CHUNKS)):
        block = size * HIDDEN
        some = pl.ds(first, size)
        rows = pl.ds(first * HIDDEN, block)
        arriving[0][c].wait()
        g = dot_nn(win[some, 0].reshape(block, WIDTH), x_ref[...])
        u = dot_nn(win[some, 1].reshape(block, WIDTH), x_ref[...])
        g_all[rows] = g.astype(BF16)
        u_all[rows] = u.astype(BF16)
        for k, (vmem, hbm) in enumerate(((g_all, g_hbm), (u_all, u_hbm))):
            copy = pltpu.make_async_copy(vmem.at[rows], hbm.at[rows], out_sems.at[k, c])
            copy.start()
            leaving.append(copy)
        active = (g * jax.nn.sigmoid(g) * u).astype(BF16).astype(F32)
        gated = (active.reshape(size, HIDDEN, TOKENS) * gate_ref[some]).astype(BF16)
        gated = gated.reshape(block, TOKENS)
        for q in range(0, size, QUAD):
            pick = one_hot_slots(place_ref[pl.ds(first + q, QUAD)])
            every = dot_nt(pick, gated[q * HIDDEN : (q + QUAD) * HIDDEN])
            for p in range(QUAD // 2):
                lanes = slice(2 * p * HIDDEN, 2 * (p + 1) * HIDDEN)
                even = every[2 * p * SLOTS : (2 * p + 1) * SLOTS, lanes]
                odd = every[(2 * p + 1) * SLOTS : (2 * p + 2) * SLOTS, lanes]
                row = ((first + q) // 2 + p) * SLOTS
                f_ref[pl.ds(row, SLOTS)] = jnp.where(lane < HIDDEN, even, odd).astype(BF16)
        arriving[1][c].wait()
        accumulate(c == 0, total, gated, wout.at[some])
    y_ref[...] = total[...].astype(BF16)
    for copy in leaving:
        copy.wait()


def vmem_spec():
    return pl.BlockSpec(memory_space=pltpu.VMEM)


def any_spec():
    return pl.BlockSpec(memory_space=pl.ANY)


def expert_scratch():
    return [
        pltpu.VMEM((EXPERTS, 2, HIDDEN, WIDTH), BF16),
        pltpu.VMEM((EXPERTS, HIDDEN, WIDTH), BF16),
        pltpu.VMEM((EXPERTS * HIDDEN, TOKENS), BF16),
        pltpu.VMEM((EXPERTS * HIDDEN, TOKENS), BF16),
        pltpu.VMEM((WIDTH, TOKENS), F32),
    ]


def expert_cost():
    return pl.CostEstimate(
        flops=6 * TOKENS * EXPERTS * HIDDEN * WIDTH, bytes_accessed=28_000_000, transcendentals=0
    )


def experts_forward(x, gates, places, w_in, w_out):
    hidden = jax.ShapeDtypeStruct((EXPERTS * HIDDEN, TOKENS), BF16)
    return pl.pallas_call(
        experts_forward_kernel,
        in_specs=[vmem_spec(), vmem_spec(), vmem_spec(), any_spec(), any_spec()],
        out_specs=[vmem_spec(), vmem_spec(), any_spec(), any_spec()],
        out_shape=[
            jax.ShapeDtypeStruct((WIDTH, TOKENS), BF16),
            jax.ShapeDtypeStruct((EXPERTS // 2 * SLOTS, 2 * HIDDEN), BF16),
            hidden,
            hidden,
        ],
        scratch_shapes=expert_scratch()
        + [pltpu.SemaphoreType.DMA((2, len(FORWARD_CHUNKS)))] * 2,
        compiler_params=pltpu.CompilerParams(vmem_limit_bytes=EXPERT_VMEM),
        cost_estimate=expert_cost(),
        name="experts_forward",
    )(x, gates, places, w_in, w_out)


def experts_backward_kernel(
    dz_ref, gate_ref, place_ref, g_hbm, u_hbm, win_hbm, wout_hbm,
    dx_ref, dgate_ref, du_ref,
    win, wout, g_all, u_all, total, in_sems,
):
    arriving = copies_in(
        (win_hbm, wout_hbm, g_hbm, u_hbm),
        (win, wout, g_all, u_all),
        in_sems,
        (1, 2, 3, 0),
        BACKWARD_CHUNKS,
    )
    for c, (first, size) in enumerate(zip(chunk_starts(BACKWARD_CHUNKS), BACKWARD_CHUNKS)):
        block = size * HIDDEN
        some = pl.ds(first, size)
        rows = pl.ds(first * HIDDEN, block)
        arriving[1][c].wait()
        through = dot_nn(wout[some].reshape(block, WIDTH), dz_ref[...])
        arriving[2][c].wait()
        arriving[3][c].wait()
        g = g_all[rows].astype(F32)
        u = u_all[rows].astype(F32)
        sig = jax.nn.sigmoid(g)
        silu = g * sig
        active = (silu * u).astype(BF16).astype(F32)
        dgate_ref[some] = jnp.sum(
            (active * through).reshape(size, HIDDEN, TOKENS), axis=1, keepdims=True
        )
        df = (through.reshape(size, HIDDEN, TOKENS) * gate_ref[some]).reshape(block, TOKENS)
        dg = (df * u * (sig * (1.0 + g * (1.0 - sig)))).astype(BF16)
        du = (df * silu).astype(BF16)
        both = jnp.concatenate(
            [dg.reshape(size, 1, HIDDEN, TOKENS), du.reshape(size, 1, HIDDEN, TOKENS)], axis=1
        ).reshape(2 * block, TOKENS)
        for q in range(0, size, QUAD):
            pick = one_hot_slots(place_ref[pl.ds(first + q, QUAD)])
            every = dot_nt(pick, both[2 * q * HIDDEN : 2 * (q + QUAD) * HIDDEN])
            for e in range(QUAD):
                du_ref[pl.ds((first + q + e) * SLOTS, SLOTS)] = every[
                    e * SLOTS : (e + 1) * SLOTS, 2 * e * HIDDEN : 2 * (e + 1) * HIDDEN
                ].astype(BF16)
        arriving[0][c].wait()
        accumulate(c == 0, total, both, win.at[some])
    dx_ref[...] = total[...].astype(BF16)


def experts_backward(dz, g, u, gates, places, w_in, w_out):
    return pl.pallas_call(
        experts_backward_kernel,
        in_specs=[vmem_spec(), vmem_spec(), vmem_spec()] + [any_spec()] * 4,
        out_specs=[vmem_spec(), vmem_spec(), vmem_spec()],
        out_shape=[
            jax.ShapeDtypeStruct((WIDTH, TOKENS), BF16),
            jax.ShapeDtypeStruct((EXPERTS, 1, TOKENS), F32),
            jax.ShapeDtypeStruct((EXPERTS * SLOTS, 2 * HIDDEN), BF16),
        ],
        scratch_shapes=expert_scratch() + [pltpu.SemaphoreType.DMA((4, len(BACKWARD_CHUNKS)))],
        compiler_params=pltpu.CompilerParams(vmem_limit_bytes=EXPERT_VMEM),
        cost_estimate=expert_cost(),
        name="experts_backward",
    )(dz, gates, places, g, u, w_in, w_out)


def slot_rows(feature_ref, place_ref):
    rows = []
    for s in range(N_SEQ):
        rows.append(dot_nt(one_hot_slots(place_ref[s]), feature_ref[s]).astype(BF16))
    return [
        jnp.concatenate([r[e * SLOTS : (e + 1) * SLOTS] for r in rows], axis=0)
        for e in range(QUAD)
    ]


def weight_grad_in_kernel(compact_ref, feature_ref, place_ref, out_ref):
    rows = slot_rows(feature_ref, place_ref)
    for e in range(QUAD):
        left = jnp.concatenate(
            [compact_ref[s, e * SLOTS : (e + 1) * SLOTS] for s in range(N_SEQ)], axis=0
        )
        out_ref[e] = dot_tn(left, rows[e])


def weight_grad_out_kernel(compact_ref, feature_ref, place_ref, out_ref):
    rows = slot_rows(feature_ref, place_ref)
    for p in range(QUAD // 2):
        left = jnp.concatenate(
            [compact_ref[s, p * SLOTS : (p + 1) * SLOTS] for s in range(N_SEQ)], axis=0
        )
        out_ref[2 * p] = dot_tn(left, rows[2 * p])[:HIDDEN]
        out_ref[2 * p + 1] = dot_tn(left, rows[2 * p + 1])[HIDDEN:]


def weight_grad(kernel, compact, feature, places, height):
    block = compact.shape[1] * QUAD // EXPERTS
    return pl.pallas_call(
        kernel,
        grid=(EXPERTS // QUAD,),
        in_specs=[
            pl.BlockSpec((N_SEQ, block, 2 * HIDDEN), lambda i: (0, i, 0)),
            pl.BlockSpec((N_SEQ, OWN, TOKENS), lambda i: (0, 0, 0)),
            pl.BlockSpec((N_SEQ, QUAD, 1, TOKENS), lambda i: (0, i, 0, 0)),
        ],
        out_specs=pl.BlockSpec((QUAD, height, OWN), lambda i: (i, 0, 0)),
        out_shape=jax.ShapeDtypeStruct((EXPERTS, height, OWN), F32),
        compiler_params=params(),
        cost_estimate=pl.CostEstimate(
            flops=2 * N_SEQ * TOKENS * EXPERTS * SLOTS * OWN, bytes_accessed=15_000_000, transcendentals=0
        ),
        name="expert_weight_grad",
    )(compact, feature, places)


def weight_grad_in(compact, feature, places):
    return weight_grad(weight_grad_in_kernel, compact, feature, places, 2 * HIDDEN)


def weight_grad_out(compact, feature, places):
    return weight_grad(weight_grad_out_kernel, compact, feature, places, HIDDEN)


def causal_mask(first):
    key = lax.broadcasted_iota(jnp.int32, (LENGTH, ROWS), 0)
    query = lax.broadcasted_iota(jnp.int32, (LENGTH, ROWS), 1) + first
    return key <= query


def side_by_side(parts):
    return jnp.concatenate(parts, axis=1)


def attention_forward_kernel(first_ref, q_ref, kv_ref, o_ref, lse_ref):
    keys = side_by_side([kv_ref[s, :HEAD_DIM] for s in range(N_SEQ)])
    values = side_by_side([kv_ref[s, HEAD_DIM:] for s in range(N_SEQ)])
    keep = causal_mask(first_ref[0])
    for h in range(PER_GROUP):
        rows = slice(h * HEAD_DIM, (h + 1) * HEAD_DIM)
        scores = jnp.where(keep, dot_tn(keys, q_ref[rows]) * SCALE, -1e30)
        top = jnp.max(scores, axis=0, keepdims=True)
        raised = jnp.exp(scores - top)
        total = jnp.sum(raised, axis=0, keepdims=True)
        probs = (raised * (1.0 / total)).astype(BF16)
        o_ref[rows] = dot_nn(values, probs).astype(BF16)
        lse_ref[h] = top + jnp.log(total)


def attention_forward(first, q, kv):
    return pl.pallas_call(
        attention_forward_kernel,
        grid=(MICRO,),
        in_specs=[
            pl.BlockSpec(memory_space=pltpu.SMEM),
            pl.BlockSpec((PER_GROUP * HEAD_DIM, ROWS), lambda m: (0, m)),
            pl.BlockSpec((N_SEQ, 2 * HEAD_DIM, ROWS), lambda m: (0, 0, m)),
        ],
        out_specs=[
            pl.BlockSpec((PER_GROUP * HEAD_DIM, ROWS), lambda m: (0, m)),
            pl.BlockSpec((PER_GROUP, 1, ROWS), lambda m: (0, 0, m)),
        ],
        out_shape=[
            jax.ShapeDtypeStruct((PER_GROUP * HEAD_DIM, TOKENS), BF16),
            jax.ShapeDtypeStruct((PER_GROUP, 1, TOKENS), F32),
        ],
        compiler_params=params(),
        name="attention_forward",
    )(first, q, kv)


def attention_backward_kernel(first_ref, q_ref, kv_ref, o_ref, do_ref, lse_ref, dq_ref, dkv_ref):
    keys = side_by_side([kv_ref[s, :HEAD_DIM] for s in range(N_SEQ)])
    values = side_by_side([kv_ref[s, HEAD_DIM:] for s in range(N_SEQ)])
    keep = causal_mask(first_ref[0])
    dkeys = jnp.zeros((HEAD_DIM, LENGTH), F32)
    dvalues = jnp.zeros((HEAD_DIM, LENGTH), F32)
    for h in range(PER_GROUP):
        rows = slice(h * HEAD_DIM, (h + 1) * HEAD_DIM)
        query = q_ref[rows]
        dout = do_ref[rows]
        scores = jnp.where(keep, dot_tn(keys, query) * SCALE, -1e30)
        probs = jnp.exp(scores - lse_ref[h])
        dvalues += dot_nt(dout, probs.astype(BF16))
        inner = jnp.sum(
            dout.astype(F32) * o_ref[rows].astype(F32), axis=0, keepdims=True
        )
        dscores = (probs * (dot_tn(values, dout) - inner)).astype(BF16)
        dkeys += dot_nt(query, dscores)
        dq_ref[rows] = dot_nn(keys, dscores) * SCALE
    dkeys = (dkeys * SCALE).astype(BF16)
    dvalues = dvalues.astype(BF16)
    for s in range(N_SEQ):
        lanes = slice(s * ROWS, (s + 1) * ROWS)
        dkv_ref[s, :HEAD_DIM] = dkeys[:, lanes]
        dkv_ref[s, HEAD_DIM:] = dvalues[:, lanes]


def attention_backward(first, q, kv, o, do, lse):
    q_spec = pl.BlockSpec((PER_GROUP * HEAD_DIM, ROWS), lambda m: (0, m))
    kv_spec = pl.BlockSpec((N_SEQ, 2 * HEAD_DIM, ROWS), lambda m: (0, 0, m))
    return pl.pallas_call(
        attention_backward_kernel,
        grid=(MICRO,),
        in_specs=[
            pl.BlockSpec(memory_space=pltpu.SMEM),
            q_spec,
            kv_spec,
            q_spec,
            q_spec,
            pl.BlockSpec((PER_GROUP, 1, ROWS), lambda m: (0, 0, m)),
        ],
        out_specs=[q_spec, kv_spec],
        out_shape=[
            jax.ShapeDtypeStruct((PER_GROUP * HEAD_DIM, TOKENS), F32),
            jax.ShapeDtypeStruct((N_SEQ, 2 * HEAD_DIM, TOKENS), BF16),
        ],
        compiler_params=params(),
        name="attention_backward",
    )(first, q, kv, o, do, lse)


def rotate(values, cosine, sine):
    half = HEAD_DIM // 2
    a, b = values[:, :half], values[:, half:]
    return jnp.concatenate([a * cosine - b * sine, b * cosine + a * sine], axis=1)


def high_low(values):
    high = values.astype(BF16)
    return high, (values - high.astype(F32)).astype(BF16)


def after(value, *others):
    return lax.optimization_barrier((value,) + others)[0]


def exchange(blocks, axis):
    return lax.all_to_all(blocks, axis, split_axis=0, concat_axis=0, tiled=False)


def summed(blocks, axis):
    return jnp.sum(exchange(blocks, axis).astype(F32), axis=0)


def on_device(
    first_layer_input,
    routes,
    cotangent,
    gains,
    qkv_weight,
    out_weight,
    router_weight,
    expert_in,
    expert_out,
):
    section_first = lax.axis_index("section") == 0
    s_index = lax.axis_index("seq")
    w_index = lax.axis_index("wa")
    first = jnp.reshape(s_index * ROWS, (1,)).astype(jnp.int32)

    def rows_of(values):
        return lax.all_gather(values, "wa", axis=0, tiled=True)

    def own(values):
        return lax.dynamic_slice_in_dim(values, w_index * OWN, OWN, 0)

    def lanes(values):
        return jnp.concatenate([values[0], values[1]], axis=1)

    def of_section(one, two):
        return jnp.where(section_first, one, two)

    x_first = lanes(first_layer_input)
    cot = lanes(cotangent)
    gain_pair = gains[0].T
    gain_high, gain_rest = high_low(gain_pair)
    gain_low = (gain_pair - gain_high.astype(F32) - gain_rest.astype(F32)).astype(BF16)
    w_qkv = qkv_weight[0]
    w_qkv_blocks = jnp.transpose(w_qkv.reshape(OWN, KV_HEADS, GROUP_COLS), (1, 0, 2))
    packed = jnp.concatenate([x_first, router_weight[0], gain_high, gain_rest, gain_low], axis=1)
    packed, w_qkv_blocks = lax.optimization_barrier((packed, w_qkv_blocks))
    w_qkv_group = exchange(w_qkv_blocks, "wa").reshape(WIDTH, GROUP_COLS)
    packed = rows_of(packed)
    x_first_full = packed[:, :TOKENS]
    w_router = packed[:, TOKENS : TOKENS + EXPERTS]
    gain_parts = packed[:, TOKENS + EXPERTS :].astype(F32)
    gain_parts = gain_parts[:, 0:2] + gain_parts[:, 2:4] + gain_parts[:, 4:6]
    gain_one, gain_two = gain_parts[:, 0:1], gain_parts[:, 1:2]
    w_attn_full = rows_of(after(out_weight[0], packed, w_qkv_group))
    w_attn_group = lax.dynamic_slice_in_dim(w_attn_full, w_index * OWN, OWN, 1)
    cot_full = rows_of(cot)
    w_in = expert_in[0]
    w_out = expert_out[0]
    own_gain_one = gains[0, 0][:, None]
    own_gain_two = gains[0, 1][:, None]

    position = (s_index * ROWS + jnp.arange(ROWS, dtype=jnp.int32)).astype(F32)
    frequency = 10000.0 ** (
        -jnp.arange(HEAD_DIM // 2).astype(F32) * (2.0 / HEAD_DIM)
    )
    angle = frequency[:, None] * position[None, :]
    cosine = jnp.tile(jnp.cos(angle), (1, MICRO))
    sine = jnp.tile(jnp.sin(angle), (1, MICRO))

    experts = jnp.arange(EXPERTS, dtype=jnp.int32)[None, :, None]
    chosen = jnp.zeros((MICRO, EXPERTS, ROWS), F32)
    for k in range(TOP):
        chosen += (routes[0][:, None, :, k] == experts).astype(F32)
    earlier = jnp.triu(jnp.ones((ROWS, ROWS), BF16), 1)
    rank = jnp.einsum("met,tu->meu", chosen.astype(BF16), earlier, preferred_element_type=F32)
    micro = jnp.arange(MICRO, dtype=jnp.int32).astype(F32)[:, None, None]
    place = lanes(jnp.where(chosen > 0.5, rank + CAP * micro, -1.0))
    chosen = lanes(chosen) > 0.5
    places = place[:, None, :]
    route_lanes = jnp.concatenate([routes[0, 0].T, routes[0, 1].T], axis=1)
    picked = (
        route_lanes[:, None, :] == jnp.arange(EXPERTS, dtype=jnp.int32)[None, :, None]
    )

    def norm_scale(values):
        return lax.rsqrt(jnp.mean(values * values, axis=0, keepdims=True) + EPSILON)

    def for_seq(blocks, shared):
        blocks = jnp.transpose(blocks.astype(BF16).reshape(OWN, N_SEQ, -1), (1, 0, 2))
        shared = jnp.concatenate(high_low(shared), axis=1)
        return jnp.concatenate(
            [blocks, jnp.broadcast_to(shared[None], (N_SEQ,) + shared.shape)], axis=2
        )

    def from_seq(blocks, n):
        total = jnp.sum(blocks.astype(F32), axis=0)
        k = (total.shape[1] - n) // 2
        return total[:, :n], total[:, n : n + k] + total[:, n + k :]

    def forward(x_own, x_full, riders):
        x = x_full.astype(F32)
        scale_one = norm_scale(x)
        normed_one = (x * scale_one * gain_one).astype(BF16)
        heads = dot_tn(w_qkv_group, normed_one).reshape(PER_GROUP + 2, HEAD_DIM, TOKENS)
        turned = rotate(heads[: PER_GROUP + 1], cosine, sine)
        turned = jnp.concatenate([turned, heads[PER_GROUP + 1 :]], axis=0).astype(BF16)
        turned = turned.reshape(GROUP_COLS, TOKENS)
        queries = turned[: PER_GROUP * HEAD_DIM]
        sent = jnp.concatenate([turned[PER_GROUP * HEAD_DIM :]] + riders, axis=0)
        key_value = exchange(jnp.broadcast_to(sent[None], (N_SEQ,) + sent.shape), "seq")
        ridden = key_value[:, 2 * HEAD_DIM :]
        key_value = key_value[:, : 2 * HEAD_DIM]
        mixed, log_total = attention_forward(first, queries, key_value)
        mixed_full = rows_of(mixed)
        middle = x + dot_nn(w_attn_full, mixed_full)
        scale_two = norm_scale(middle)
        normed_two = (middle * scale_two * gain_two).astype(BF16)
        logits = dot_tn(w_router, normed_two)
        raised = jnp.where(
            chosen,
            jnp.exp(logits - jnp.max(jnp.where(chosen, logits, -1e30), axis=0, keepdims=True)),
            0.0,
        )
        gates = raised / jnp.sum(raised, axis=0, keepdims=True)
        part, compact, g, u = experts_forward(
            normed_two, gates[:, None, :], places, w_in, w_out
        )
        out = own(middle) + summed(part.reshape(N_WA, OWN, TOKENS), "wa")
        saved = (
            x_own,
            scale_one,
            own(normed_one),
            queries,
            key_value,
            log_total,
            mixed,
            mixed_full,
            middle,
            scale_two,
            normed_two,
            logits,
            gates,
            g,
            u,
        )
        return out.astype(BF16), compact, saved, ridden

    def backward(dz, dz_full, saved, alongside, later):
        (
            x_own,
            scale_one,
            own_normed_one,
            queries,
            key_value,
            log_total,
            mixed,
            mixed_full,
            middle,
            scale_two,
            normed_two,
            logits,
            gates,
            g,
            u,
        ) = saved
        part, dgate, du = experts_backward(
            dz_full, g, u, gates[:, None, :], places, w_in, w_out
        )
        part, alongside = lax.optimization_barrier((part, alongside))
        if later is not None:
            du = of_section(du, later[0])
            part, du = lax.optimization_barrier((part, du))
        inner = jnp.sum(part.astype(F32) * middle * gain_two, axis=0, keepdims=True)
        dgate_top = jnp.sum(jnp.where(picked, dgate[:, 0][None], 0.0), axis=1)
        extra = jnp.concatenate(
            [
                dgate_top.astype(BF16),
                *high_low(inner),
                jnp.zeros((16 - TOP - 2, TOKENS), BF16),
            ],
            axis=0,
        )
        blocks = jnp.concatenate(
            [
                part.reshape(N_WA, OWN, TOKENS),
                jnp.broadcast_to(extra[None], (N_WA, 16, TOKENS)),
            ],
            axis=1,
        )
        back = exchange(blocks, "wa")
        if later is not None:
            expert_out_grad = weight_grad_out(compact_out, alongside, places_all)
            back, expert_out_grad = lax.optimization_barrier((back, expert_out_grad))
        back = jnp.sum(back.astype(F32), axis=0)
        dgate_top = back[OWN : OWN + TOP]
        inner = back[OWN + TOP : OWN + TOP + 1] + back[OWN + TOP + 1 : OWN + TOP + 2]
        dgate = jnp.sum(jnp.where(picked, dgate_top[:, None, :], 0.0), axis=0)
        dlogit = gates * (dgate - jnp.sum(gates * dgate, axis=0, keepdims=True))
        dlogit_high, dlogit_low = high_low(dlogit)
        own_router = router_weight[0]
        dnormed = back[:OWN] + dot_nn(own_router, dlogit_high) + dot_nn(own_router, dlogit_low)
        inner += jnp.sum(dlogit * logits, axis=0, keepdims=True) / scale_two
        own_middle = own(middle)
        dmiddle = (
            dz.astype(F32)
            + scale_two * own_gain_two * dnormed
            - own_middle * (scale_two * scale_two * scale_two * inner * (1.0 / WIDTH))
        )
        gain_two_grad = jnp.sum(dnormed * own_middle * scale_two, axis=1, keepdims=True)
        own_normed_two = own(normed_two)
        router_grad = dot_nt(own_normed_two, dlogit_high) + dot_nt(own_normed_two, dlogit_low)
        dmiddle_low = dmiddle.astype(BF16)
        attn_grad = dot_nt(dmiddle_low, mixed_full)
        small_grad = jnp.concatenate([gain_two_grad, router_grad], axis=1)
        if later is not None:
            blocks = for_seq(of_section(attn_grad, later[1]), of_section(small_grad, later[2]))
            dmiddle_low, blocks = lax.optimization_barrier((dmiddle_low, blocks))
            attn_grad = exchange(blocks, "seq")
        dmiddle_full = rows_of(dmiddle_low)
        if later is not None:
            dmiddle_full, attn_grad = lax.optimization_barrier((dmiddle_full, attn_grad))
            attn_grad, small_grad = from_seq(attn_grad, OWN)
        dmixed = dot_tn(w_attn_group, dmiddle_full).astype(BF16)
        dq, dkv = attention_backward(first, queries, key_value, mixed, dmixed, log_total)
        dkv = summed(dkv, "seq")
        dturned = jnp.concatenate([dq, dkv], axis=0)
        turned = jnp.concatenate(
            [queries, lax.dynamic_index_in_dim(key_value, s_index, 0, False)], axis=0
        )
        inner_one = jnp.sum(dturned * turned.astype(F32), axis=0, keepdims=True)
        dheads = dturned.reshape(PER_GROUP + 2, HEAD_DIM, TOKENS)
        dheads = jnp.concatenate(
            [rotate(dheads[: PER_GROUP + 1], cosine, -sine), dheads[PER_GROUP + 1 :]], axis=0
        )
        sent = jnp.concatenate(
            [
                dheads.reshape(GROUP_COLS, TOKENS).astype(BF16),
                *high_low(inner_one),
                jnp.zeros((14, TOKENS), BF16),
            ],
            axis=0,
        )
        full = exchange(jnp.broadcast_to(sent[None], (N_WA,) + sent.shape), "wa")
        dheads_full = full[:, :GROUP_COLS].reshape(KV_HEADS * GROUP_COLS, TOKENS)
        inner_one = jnp.sum(
            full[:, GROUP_COLS : GROUP_COLS + 2].astype(F32), axis=(0, 1)
        )[None] / scale_one
        dnormed_one = dot_nn(w_qkv, dheads_full)
        x = x_own.astype(F32)
        dx = (
            dmiddle
            + scale_one * own_gain_one * dnormed_one
            - x * (scale_one * scale_one * scale_one * inner_one * (1.0 / WIDTH))
        )
        gain_one_grad = jnp.sum(dnormed_one * x * scale_one, axis=1, keepdims=True)
        qkv_grad = dot_nt(own_normed_one, dheads_full)
        if later is None:
            return dx, alongside, (du, attn_grad, small_grad, gain_one_grad, qkv_grad)
        blocks = for_seq(of_section(qkv_grad, later[4]), of_section(gain_one_grad, later[3]))
        qkv_grad, gain_one_grad = from_seq(exchange(blocks, "seq"), GROUP_COLS)
        return dx, expert_out_grad, (du, attn_grad, small_grad, gain_one_grad, qkv_grad)

    riders = [jnp.concatenate([place, jnp.zeros((8, TOKENS), F32)], axis=0).astype(BF16)]
    out_one, compact_one, saved_one, ridden = forward(x_first, x_first_full, riders)
    places_all = ridden[:, :EXPERTS].astype(F32)[:, :, None, :]
    received = lax.ppermute(out_one, "section", [(0, 1)])
    out_two, compact_two, saved_two, _ = forward(received, rows_of(received), [])

    feature_in = exchange(
        of_section(saved_one[10], saved_two[10]).reshape(N_SEQ, OWN, TOKENS), "seq"
    )
    compact_out = lax.all_gather(of_section(compact_one, compact_two), "seq", axis=0, tiled=False)

    back_two = backward(cot, cot_full, saved_two, feature_in, None)
    feature_in = back_two[1]
    returned = lax.ppermute(
        after(back_two[0].astype(BF16), compact_out), "section", [(1, 0)]
    )
    returned_full = rows_of(returned)
    feature_out = exchange(
        of_section(returned_full, cot_full).reshape(N_SEQ, OWN, TOKENS), "seq"
    )
    back_one = backward(returned, returned_full, saved_one, feature_out, back_two[2])
    expert_out_grad = back_one[1]
    compact_in, attn_grad, small_grad, gain_one_grad, qkv_grad = back_one[2]
    compact_in = lax.all_gather(compact_in, "seq", axis=0, tiled=False)
    expert_in_grad = weight_grad_in(compact_in, feature_in, places_all)

    def tokens_first(values):
        return jnp.transpose(values.reshape(OWN, MICRO, ROWS), (1, 2, 0))[None]

    return (
        tokens_first(of_section(out_one, out_two)),
        tokens_first(of_section(back_one[0], back_two[0])),
        jnp.stack([gain_one_grad[:, 0], small_grad[:, 0]])[None],
        qkv_grad[None],
        attn_grad[None],
        small_grad[None, :, 1:],
        expert_in_grad.reshape(1, EXPERTS, 2, HIDDEN, OWN),
        expert_out_grad[None],
    )


def solution(mesh):
    return jax.shard_map(
        on_device,
        mesh=mesh,
        in_specs=(
            P(None, "wa", "seq"),
            P("section", None, "seq", None),
            P(None, "wa", "seq"),
            P("section", None, "wa"),
            P("section", "wa", None),
            P("section", "wa", None),
            P("section", "wa", None),
            P("section", None, None, "wa", None),
            P("section", None, "wa", None),
        ),
        out_specs=(
            P("section", None, "seq", "wa"),
            P("section", None, "seq", "wa"),
            P("section", None, "wa"),
            P("section", "wa", "seq"),
            P("section", "wa", "seq"),
            P("section", "wa", None),
            P("section", None, None, "wa", "seq"),
            P("section", None, "wa", "seq"),
        ),
        check_vma=False,
    )
```

```python
import jax
import jax.numpy as jnp
from jax import lax
from jax.experimental import pallas as pl
from jax.experimental.pallas import tpu as pltpu
from jax.sharding import PartitionSpec as P

HEADS = 24
KV_HEADS = 8
PER_GROUP = HEADS // KV_HEADS
HEAD_DIM = 64
EXPERTS = 40
TOP = 8
MICRO = 2
CAP = 32
N_SEQ = 8
N_WA = 8
ROWS = 128
WIDTH = 1536
OWN = WIDTH // N_WA
TOKENS = MICRO * ROWS
LENGTH = ROWS * N_SEQ
HIDDEN = 64
SLOTS = MICRO * CAP
GROUP_COLS = (PER_GROUP + 2) * HEAD_DIM
BATCH = 8
STEPS = EXPERTS // BATCH
BLOCK = BATCH * HIDDEN
QUAD = 4
COLUMNS = 256
ATTN_CHUNKS = 4
EXTRA = 16
SCALE = HEAD_DIM ** (-0.5)
EPSILON = 1e-06
BF16 = jnp.bfloat16
F32 = jnp.float32
VMEM_LIMIT = 58 * 1024 * 1024
EXPERT_VMEM = 58 * 1024 * 1024


def dot_nn(a, b):
    return lax.dot_general(a, b, (((1,), (0,)), ((), ())), preferred_element_type=F32)


def dot_nt(a, b):
    return lax.dot_general(a, b, (((1,), (1,)), ((), ())), preferred_element_type=F32)


def dot_tn(a, b):
    return lax.dot_general(a, b, (((0,), (0,)), ((), ())), preferred_element_type=F32)


def params():
    return pltpu.CompilerParams(
        vmem_limit_bytes=VMEM_LIMIT, dimension_semantics=("arbitrary",)
    )


def one_hot_slots(places):
    slot = lax.broadcasted_iota(jnp.int32, (QUAD, SLOTS, TOKENS), 1).astype(F32)
    hit = jnp.where(slot == places, 1.0, 0.0)
    return hit.reshape(QUAD * SLOTS, TOKENS).astype(BF16)


def copied(pairs, sems):
    copies = []
    for k, (source, target) in enumerate(pairs):
        copy = pltpu.make_async_copy(source, target, sems.at[k])
        copy.start()
        copies.append(copy)
    return copies


def chunk_copies(pairs, sems, c):
    copies = []
    for k, (source, target) in enumerate(pairs):
        rows = source.shape[0] // STEPS
        part = pl.ds(pl.multiple_of(c * rows, rows), rows)
        copies.append(pltpu.make_async_copy(source.at[part], target.at[part], sems.at[k, c]))
    return copies


def start_chunks(pairs, sems):
    @pl.loop(0, STEPS)
    def _(c):
        for copy in chunk_copies(pairs, sems, c):
            copy.start()


def accumulate(total, left, right_ref):
    for c in range(0, WIDTH, COLUMNS):
        cols = slice(c, c + COLUMNS)
        total[cols] += dot_tn(right_ref[..., cols].reshape(left.shape[0], COLUMNS), left)


def experts_forward_kernel(
    x_hbm, mixed_hbm, gain_hbm, router_hbm, chosen_hbm, place_hbm, wattn_hbm, win_hbm, wout_hbm,
    y_ref, f_ref, scale_ref, logit_ref, gate_ref, middle_hbm, normed_hbm, g_hbm, u_hbm,
    x_ref, mixed_ref, gain_ref, router_ref, chosen_ref, place_ref, middle_ref, normed_ref,
    gate_rows, wattn, win, wout, g_all, u_all, total, small_sems, attn_sems, in_sems, out_sems,
):
    height = WIDTH // ATTN_CHUNKS
    mixed_copy, x_copy = copied(((mixed_hbm, mixed_ref), (x_hbm, x_ref)), small_sems)
    attn = [
        pltpu.make_async_copy(
            wattn_hbm.at[pl.ds(c * height, height)], wattn.at[pl.ds(c * height, height)], attn_sems.at[c]
        )
        for c in range(ATTN_CHUNKS)
    ]
    for copy in attn:
        copy.start()
    small = copied(
        (
            (gain_hbm, gain_ref),
            (router_hbm, router_ref),
            (chosen_hbm, chosen_ref),
            (place_hbm, place_ref),
        ),
        small_sems.at[pl.ds(2, 4)],
    )
    weights = ((win_hbm, win), (wout_hbm, wout))
    start_chunks(weights, in_sems)
    total[...] = jnp.zeros_like(total)
    mixed_copy.wait()
    x_copy.wait()

    squares = jnp.zeros((1, TOKENS), F32)
    for c in range(ATTN_CHUNKS):
        part = pl.ds(c * height, height)
        attn[c].wait()
        middle = x_ref[part].astype(F32) + dot_nn(wattn[part], mixed_ref[...])
        middle_ref[part] = middle
        squares += jnp.sum(middle * middle, axis=0, keepdims=True)
    scale = lax.rsqrt(squares * (1.0 / WIDTH) + EPSILON)
    scale_ref[...] = scale
    for copy in small:
        copy.wait()
    normed_ref[...] = (middle_ref[...] * scale * gain_ref[...]).astype(BF16)
    logits = dot_tn(router_ref[...], normed_ref[...])
    logit_ref[...] = logits
    chosen = chosen_ref[...] > 0.5
    top = jnp.max(jnp.where(chosen, logits, -1e30), axis=0, keepdims=True)
    raised = jnp.where(chosen, jnp.exp(jnp.where(chosen, logits - top, 0.0)), 0.0)
    gates = raised / jnp.sum(raised, axis=0, keepdims=True)
    gate_ref[...] = gates
    for e in range(EXPERTS):
        gate_rows[e] = gates[e : e + 1]

    leaving = copied(
        ((middle_ref, middle_hbm), (normed_ref, normed_hbm)), small_sems.at[pl.ds(6, 2)]
    )
    lane = lax.broadcasted_iota(jnp.int32, (SLOTS, 2 * HIDDEN), 1)
    hidden = ((g_all, g_hbm), (u_all, u_hbm))

    @pl.loop(0, STEPS)
    def _(c):
        some = pl.ds(c * BATCH, BATCH)
        rows = pl.ds(pl.multiple_of(c * BLOCK, BLOCK), BLOCK)
        win_copy, wout_copy = chunk_copies(weights, in_sems, c)
        win_copy.wait()
        g = dot_nn(win[some, 0].reshape(BLOCK, WIDTH), normed_ref[...])
        u = dot_nn(win[some, 1].reshape(BLOCK, WIDTH), normed_ref[...])
        g_all[rows] = g.astype(BF16)
        u_all[rows] = u.astype(BF16)
        for copy in chunk_copies(hidden, out_sems, c):
            copy.start()
        active = (g * jax.nn.sigmoid(g) * u).astype(BF16).astype(F32)
        gated = (active.reshape(BATCH, HIDDEN, TOKENS) * gate_rows[some]).astype(BF16)
        gated = gated.reshape(BLOCK, TOKENS)
        for q in range(0, BATCH, QUAD):
            pick = one_hot_slots(place_ref[pl.ds(c * BATCH + q, QUAD)])
            every = dot_nt(pick, gated[q * HIDDEN : (q + QUAD) * HIDDEN])
            for p in range(QUAD // 2):
                lanes = slice(2 * p * HIDDEN, 2 * (p + 1) * HIDDEN)
                even = every[2 * p * SLOTS : (2 * p + 1) * SLOTS, lanes]
                odd = every[(2 * p + 1) * SLOTS : (2 * p + 2) * SLOTS, lanes]
                row = pl.multiple_of((c * BATCH + q) // 2 * SLOTS + p * SLOTS, SLOTS)
                f_ref[pl.ds(row, SLOTS)] = jnp.where(lane < HIDDEN, even, odd).astype(BF16)
        wout_copy.wait()
        accumulate(total, gated, wout.at[some])

    y_ref[...] = total[...].astype(BF16)
    for copy in leaving:
        copy.wait()

    @pl.loop(0, STEPS)
    def _(c):
        for copy in chunk_copies(hidden, out_sems, c):
            copy.wait()


def vmem_spec():
    return pl.BlockSpec(memory_space=pltpu.VMEM)


def any_spec():
    return pl.BlockSpec(memory_space=pl.ANY)


def expert_scratch():
    return [
        pltpu.VMEM((EXPERTS, 2, HIDDEN, WIDTH), BF16),
        pltpu.VMEM((EXPERTS, HIDDEN, WIDTH), BF16),
        pltpu.VMEM((EXPERTS * HIDDEN, TOKENS), BF16),
        pltpu.VMEM((EXPERTS * HIDDEN, TOKENS), BF16),
        pltpu.VMEM((WIDTH, TOKENS), F32),
    ]


def expert_cost():
    return pl.CostEstimate(
        flops=6 * TOKENS * EXPERTS * HIDDEN * WIDTH, bytes_accessed=28_000_000, transcendentals=0
    )


def experts_forward(x, mixed, gain, router, chosen, places, w_attn, w_in, w_out):
    hidden = jax.ShapeDtypeStruct((EXPERTS * HIDDEN, TOKENS), BF16)
    some = jax.ShapeDtypeStruct((EXPERTS, TOKENS), F32)
    return pl.pallas_call(
        experts_forward_kernel,
        in_specs=[any_spec()] * 9,
        out_specs=[vmem_spec()] * 5 + [any_spec()] * 4,
        out_shape=[
            jax.ShapeDtypeStruct((WIDTH, TOKENS), BF16),
            jax.ShapeDtypeStruct((EXPERTS // 2 * SLOTS, 2 * HIDDEN), BF16),
            jax.ShapeDtypeStruct((1, TOKENS), F32),
            some,
            some,
            jax.ShapeDtypeStruct((WIDTH, TOKENS), F32),
            jax.ShapeDtypeStruct((WIDTH, TOKENS), BF16),
            hidden,
            hidden,
        ],
        scratch_shapes=[
            pltpu.VMEM((WIDTH, TOKENS), BF16),
            pltpu.VMEM((WIDTH, TOKENS), BF16),
            pltpu.VMEM((WIDTH, 1), F32),
            pltpu.VMEM((WIDTH, EXPERTS), BF16),
            pltpu.VMEM((EXPERTS, TOKENS), F32),
            pltpu.VMEM((EXPERTS, 1, TOKENS), F32),
            pltpu.VMEM((WIDTH, TOKENS), F32),
            pltpu.VMEM((WIDTH, TOKENS), BF16),
            pltpu.VMEM((EXPERTS, 1, TOKENS), F32),
            pltpu.VMEM((WIDTH, WIDTH), BF16),
        ]
        + expert_scratch()
        + [pltpu.SemaphoreType.DMA((8,)), pltpu.SemaphoreType.DMA((ATTN_CHUNKS,))]
        + [pltpu.SemaphoreType.DMA((2, STEPS))] * 2,
        compiler_params=pltpu.CompilerParams(vmem_limit_bytes=EXPERT_VMEM),
        cost_estimate=expert_cost(),
        name="experts_forward",
    )(x, mixed, gain, router, chosen, places, w_attn, w_in, w_out)


def experts_backward_kernel(
    dz_hbm, gain_hbm, gate_hbm, place_hbm, route_hbm,
    g_hbm, u_hbm, middle_hbm, win_hbm, wout_hbm,
    out_ref, du_ref,
    dz_ref, gain_ref, gate_ref, place_ref, route_ref,
    win, wout, g_all, u_all, total, middle_all, dgate_all, in_sems, small_sems,
):
    dz_copy, gate_copy, place_copy = copied(
        ((dz_hbm, dz_ref), (gate_hbm, gate_ref), (place_hbm, place_ref)), small_sems
    )
    pairs = ((wout_hbm, wout), (g_hbm, g_all), (u_hbm, u_all), (win_hbm, win))
    start_chunks(pairs, in_sems)
    total[...] = jnp.zeros_like(total)
    late = copied(
        ((middle_hbm, middle_all), (gain_hbm, gain_ref), (route_hbm, route_ref)),
        small_sems.at[pl.ds(3, 3)],
    )
    dz_copy.wait()
    gate_copy.wait()
    place_copy.wait()

    @pl.loop(0, STEPS)
    def _(c):
        some = pl.ds(c * BATCH, BATCH)
        rows = pl.ds(pl.multiple_of(c * BLOCK, BLOCK), BLOCK)
        wout_copy, g_copy, u_copy, win_copy = chunk_copies(pairs, in_sems, c)
        wout_copy.wait()
        through = dot_nn(wout[some].reshape(BLOCK, WIDTH), dz_ref[...])
        g_copy.wait()
        u_copy.wait()
        g = g_all[rows].astype(F32)
        u = u_all[rows].astype(F32)
        sig = jax.nn.sigmoid(g)
        silu = g * sig
        active = (silu * u).astype(BF16).astype(F32)
        dgate_all[pl.ds(pl.multiple_of(c * BATCH, BATCH), BATCH)] = jnp.sum(
            (active * through).reshape(BATCH, HIDDEN, TOKENS), axis=1
        )
        df = (through.reshape(BATCH, HIDDEN, TOKENS) * gate_ref[some]).reshape(BLOCK, TOKENS)
        dg = (df * u * (sig * (1.0 + g * (1.0 - sig)))).astype(BF16)
        du = (df * silu).astype(BF16)
        both = jnp.concatenate(
            [dg.reshape(BATCH, 1, HIDDEN, TOKENS), du.reshape(BATCH, 1, HIDDEN, TOKENS)], axis=1
        ).reshape(2 * BLOCK, TOKENS)
        for q in range(0, BATCH, QUAD):
            pick = one_hot_slots(place_ref[pl.ds(c * BATCH + q, QUAD)])
            every = dot_nt(pick, both[2 * q * HIDDEN : 2 * (q + QUAD) * HIDDEN])
            for e in range(QUAD):
                row = pl.multiple_of((c * BATCH + q + e) * SLOTS, SLOTS)
                du_ref[pl.ds(row, SLOTS)] = every[
                    e * SLOTS : (e + 1) * SLOTS, 2 * e * HIDDEN : 2 * (e + 1) * HIDDEN
                ].astype(BF16)
        win_copy.wait()
        accumulate(total, both, win.at[some])

    for copy in late:
        copy.wait()
    inner = jnp.zeros((1, TOKENS), F32)
    for w in range(N_WA):
        part = pl.ds(w * OWN, OWN)
        share = total[part].astype(BF16)
        out_ref[w, :OWN] = share
        inner += jnp.sum(
            share.astype(F32) * middle_all[part] * gain_ref[part], axis=0, keepdims=True
        )
    expert = lax.broadcasted_iota(jnp.int32, (EXPERTS, TOKENS), 0)
    dgate = dgate_all[...]
    tops = [
        jnp.sum(jnp.where(expert == route_ref[k : k + 1], dgate, 0.0), axis=0, keepdims=True)
        for k in range(TOP)
    ]
    high = inner.astype(BF16).astype(F32)
    extra = jnp.concatenate(
        tops + [high, inner - high, jnp.zeros((EXTRA - TOP - 2, TOKENS), F32)], axis=0
    ).astype(BF16)
    for w in range(N_WA):
        out_ref[w, OWN:] = extra


def experts_backward(dz, gain, gates, places, routes, g, u, middle, w_in, w_out):
    return pl.pallas_call(
        experts_backward_kernel,
        in_specs=[any_spec()] * 10,
        out_specs=[vmem_spec()] * 2,
        out_shape=[
            jax.ShapeDtypeStruct((N_WA, OWN + EXTRA, TOKENS), BF16),
            jax.ShapeDtypeStruct((EXPERTS * SLOTS, 2 * HIDDEN), BF16),
        ],
        scratch_shapes=[
            pltpu.VMEM((WIDTH, TOKENS), BF16),
            pltpu.VMEM((WIDTH, 1), F32),
            pltpu.VMEM((EXPERTS, 1, TOKENS), F32),
            pltpu.VMEM((EXPERTS, 1, TOKENS), F32),
            pltpu.VMEM((TOP, TOKENS), jnp.int32),
        ]
        + expert_scratch()
        + [
            pltpu.VMEM((WIDTH, TOKENS), F32),
            pltpu.VMEM((EXPERTS, TOKENS), F32),
            pltpu.SemaphoreType.DMA((4, STEPS)),
            pltpu.SemaphoreType.DMA((6,)),
        ],
        compiler_params=pltpu.CompilerParams(vmem_limit_bytes=EXPERT_VMEM),
        cost_estimate=expert_cost(),
        name="experts_backward",
    )(dz, gain, gates, places, routes, g, u, middle, w_in, w_out)


def slot_rows(feature_ref, place_ref):
    rows = []
    for s in range(N_SEQ):
        rows.append(dot_nt(one_hot_slots(place_ref[s]), feature_ref[s]).astype(BF16))
    return [
        jnp.concatenate([r[e * SLOTS : (e + 1) * SLOTS] for r in rows], axis=0)
        for e in range(QUAD)
    ]


def weight_grad_in_kernel(compact_ref, feature_ref, place_ref, out_ref):
    rows = slot_rows(feature_ref, place_ref)
    for e in range(QUAD):
        left = jnp.concatenate(
            [compact_ref[s, e * SLOTS : (e + 1) * SLOTS] for s in range(N_SEQ)], axis=0
        )
        out_ref[e] = dot_tn(left, rows[e])


def weight_grad_out_kernel(compact_ref, feature_ref, place_ref, out_ref):
    rows = slot_rows(feature_ref, place_ref)
    for p in range(QUAD // 2):
        left = jnp.concatenate(
            [compact_ref[s, p * SLOTS : (p + 1) * SLOTS] for s in range(N_SEQ)], axis=0
        )
        out_ref[2 * p] = dot_tn(left, rows[2 * p])[:HIDDEN]
        out_ref[2 * p + 1] = dot_tn(left, rows[2 * p + 1])[HIDDEN:]


def weight_grad(kernel, compact, feature, places, height):
    block = compact.shape[1] * QUAD // EXPERTS
    return pl.pallas_call(
        kernel,
        grid=(EXPERTS // QUAD,),
        in_specs=[
            pl.BlockSpec((N_SEQ, block, 2 * HIDDEN), lambda i: (0, i, 0)),
            pl.BlockSpec((N_SEQ, OWN, TOKENS), lambda i: (0, 0, 0)),
            pl.BlockSpec((N_SEQ, QUAD, 1, TOKENS), lambda i: (0, i, 0, 0)),
        ],
        out_specs=pl.BlockSpec((QUAD, height, OWN), lambda i: (i, 0, 0)),
        out_shape=jax.ShapeDtypeStruct((EXPERTS, height, OWN), F32),
        compiler_params=params(),
        cost_estimate=pl.CostEstimate(
            flops=2 * N_SEQ * TOKENS * EXPERTS * SLOTS * OWN, bytes_accessed=15_000_000, transcendentals=0
        ),
        name="expert_weight_grad",
    )(compact, feature, places)


def weight_grad_in(compact, feature, places):
    return weight_grad(weight_grad_in_kernel, compact, feature, places, 2 * HIDDEN)


def weight_grad_out(compact, feature, places):
    return weight_grad(weight_grad_out_kernel, compact, feature, places, HIDDEN)


def causal_mask(first):
    key = lax.broadcasted_iota(jnp.int32, (LENGTH, ROWS), 0)
    query = lax.broadcasted_iota(jnp.int32, (LENGTH, ROWS), 1) + first
    return key <= query


def side_by_side(parts):
    return jnp.concatenate(parts, axis=1)


def attention_forward_kernel(first_ref, q_ref, kv_ref, o_ref, lse_ref):
    keys = side_by_side([kv_ref[s, :HEAD_DIM] for s in range(N_SEQ)])
    values = side_by_side([kv_ref[s, HEAD_DIM:] for s in range(N_SEQ)])
    keep = causal_mask(first_ref[0])
    for h in range(PER_GROUP):
        rows = slice(h * HEAD_DIM, (h + 1) * HEAD_DIM)
        scores = jnp.where(keep, dot_tn(keys, q_ref[rows]) * SCALE, -1e30)
        top = jnp.max(scores, axis=0, keepdims=True)
        raised = jnp.exp(scores - top)
        total = jnp.sum(raised, axis=0, keepdims=True)
        probs = (raised * (1.0 / total)).astype(BF16)
        o_ref[rows] = dot_nn(values, probs).astype(BF16)
        lse_ref[h] = top + jnp.log(total)


def attention_forward(first, q, kv):
    return pl.pallas_call(
        attention_forward_kernel,
        grid=(MICRO,),
        in_specs=[
            pl.BlockSpec(memory_space=pltpu.SMEM),
            pl.BlockSpec((PER_GROUP * HEAD_DIM, ROWS), lambda m: (0, m)),
            pl.BlockSpec((N_SEQ, 2 * HEAD_DIM, ROWS), lambda m: (0, 0, m)),
        ],
        out_specs=[
            pl.BlockSpec((PER_GROUP * HEAD_DIM, ROWS), lambda m: (0, m)),
            pl.BlockSpec((PER_GROUP, 1, ROWS), lambda m: (0, 0, m)),
        ],
        out_shape=[
            jax.ShapeDtypeStruct((PER_GROUP * HEAD_DIM, TOKENS), BF16),
            jax.ShapeDtypeStruct((PER_GROUP, 1, TOKENS), F32),
        ],
        compiler_params=params(),
        name="attention_forward",
    )(first, q, kv)


def attention_backward_kernel(first_ref, q_ref, kv_ref, o_ref, do_ref, lse_ref, dq_ref, dkv_ref):
    keys = side_by_side([kv_ref[s, :HEAD_DIM] for s in range(N_SEQ)])
    values = side_by_side([kv_ref[s, HEAD_DIM:] for s in range(N_SEQ)])
    keep = causal_mask(first_ref[0])
    dkeys = jnp.zeros((HEAD_DIM, LENGTH), F32)
    dvalues = jnp.zeros((HEAD_DIM, LENGTH), F32)
    for h in range(PER_GROUP):
        rows = slice(h * HEAD_DIM, (h + 1) * HEAD_DIM)
        query = q_ref[rows]
        dout = do_ref[rows]
        scores = jnp.where(keep, dot_tn(keys, query) * SCALE, -1e30)
        probs = jnp.exp(scores - lse_ref[h])
        dvalues += dot_nt(dout, probs.astype(BF16))
        inner = jnp.sum(
            dout.astype(F32) * o_ref[rows].astype(F32), axis=0, keepdims=True
        )
        dscores = (probs * (dot_tn(values, dout) - inner)).astype(BF16)
        dkeys += dot_nt(query, dscores)
        dq_ref[rows] = dot_nn(keys, dscores) * SCALE
    dkeys = (dkeys * SCALE).astype(BF16)
    dvalues = dvalues.astype(BF16)
    for s in range(N_SEQ):
        lanes = slice(s * ROWS, (s + 1) * ROWS)
        dkv_ref[s, :HEAD_DIM] = dkeys[:, lanes]
        dkv_ref[s, HEAD_DIM:] = dvalues[:, lanes]


def attention_backward(first, q, kv, o, do, lse):
    q_spec = pl.BlockSpec((PER_GROUP * HEAD_DIM, ROWS), lambda m: (0, m))
    kv_spec = pl.BlockSpec((N_SEQ, 2 * HEAD_DIM, ROWS), lambda m: (0, 0, m))
    return pl.pallas_call(
        attention_backward_kernel,
        grid=(MICRO,),
        in_specs=[
            pl.BlockSpec(memory_space=pltpu.SMEM),
            q_spec,
            kv_spec,
            q_spec,
            q_spec,
            pl.BlockSpec((PER_GROUP, 1, ROWS), lambda m: (0, 0, m)),
        ],
        out_specs=[q_spec, kv_spec],
        out_shape=[
            jax.ShapeDtypeStruct((PER_GROUP * HEAD_DIM, TOKENS), F32),
            jax.ShapeDtypeStruct((N_SEQ, 2 * HEAD_DIM, TOKENS), BF16),
        ],
        compiler_params=params(),
        name="attention_backward",
    )(first, q, kv, o, do, lse)


def rotate(values, cosine, sine):
    half = HEAD_DIM // 2
    a, b = values[:, :half], values[:, half:]
    return jnp.concatenate([a * cosine - b * sine, b * cosine + a * sine], axis=1)


def high_low(values):
    high = lax.reduce_precision(values, 8, 7)
    return high.astype(BF16), (values - high).astype(BF16)


def after(value, *others):
    return lax.optimization_barrier((value,) + others)[0]


def exchange(blocks, axis):
    return lax.all_to_all(blocks, axis, split_axis=0, concat_axis=0, tiled=False)


def summed(blocks, axis):
    return jnp.sum(exchange(blocks, axis).astype(F32), axis=0)


def on_device(
    first_layer_input,
    routes,
    cotangent,
    gains,
    qkv_weight,
    out_weight,
    router_weight,
    expert_in,
    expert_out,
):
    section_first = lax.axis_index("section") == 0
    s_index = lax.axis_index("seq")
    w_index = lax.axis_index("wa")
    first = jnp.reshape(s_index * ROWS, (1,)).astype(jnp.int32)

    def rows_of(values):
        return lax.all_gather(values, "wa", axis=0, tiled=True)

    def own(values):
        return lax.dynamic_slice_in_dim(values, w_index * OWN, OWN, 0)

    def lanes(values):
        return jnp.concatenate([values[0], values[1]], axis=1)

    def of_section(one, two):
        return jnp.where(section_first, one, two)

    x_first = lanes(first_layer_input)
    cot = lanes(cotangent)
    gain_pair = gains[0].T
    gain_high = lax.reduce_precision(gain_pair, 8, 7)
    gain_rest, gain_low = high_low(gain_pair - gain_high)
    gain_high = gain_high.astype(BF16)
    w_qkv = qkv_weight[0]
    w_qkv_blocks = jnp.transpose(w_qkv.reshape(OWN, KV_HEADS, GROUP_COLS), (1, 0, 2))
    packed = jnp.concatenate([x_first, router_weight[0], gain_high, gain_rest, gain_low], axis=1)
    packed, w_qkv_blocks = lax.optimization_barrier((packed, w_qkv_blocks))
    w_qkv_group = exchange(w_qkv_blocks, "wa").reshape(WIDTH, GROUP_COLS)
    packed = rows_of(packed)
    x_first_full = packed[:, :TOKENS]
    w_router = packed[:, TOKENS : TOKENS + EXPERTS]
    gain_parts = packed[:, TOKENS + EXPERTS :].astype(F32)
    gain_parts = gain_parts[:, 0:2] + gain_parts[:, 2:4] + gain_parts[:, 4:6]
    gain_one, gain_two = gain_parts[:, 0:1], gain_parts[:, 1:2]
    w_attn_full = rows_of(after(out_weight[0], packed, w_qkv_group))
    w_attn_group = lax.dynamic_slice_in_dim(w_attn_full, w_index * OWN, OWN, 1)
    cot_full = rows_of(cot)
    w_in = expert_in[0]
    w_out = expert_out[0]
    own_gain_one = gains[0, 0][:, None]
    own_gain_two = gains[0, 1][:, None]

    position = (s_index * ROWS + jnp.arange(ROWS, dtype=jnp.int32)).astype(F32)
    frequency = 10000.0 ** (
        -jnp.arange(HEAD_DIM // 2).astype(F32) * (2.0 / HEAD_DIM)
    )
    angle = frequency[:, None] * position[None, :]
    cosine = jnp.tile(jnp.cos(angle), (1, MICRO))
    sine = jnp.tile(jnp.sin(angle), (1, MICRO))

    experts = jnp.arange(EXPERTS, dtype=jnp.int32)[None, :, None]
    chosen = jnp.zeros((MICRO, EXPERTS, ROWS), F32)
    for k in range(TOP):
        chosen += (routes[0][:, None, :, k] == experts).astype(F32)
    earlier = jnp.triu(jnp.ones((ROWS, ROWS), BF16), 1)
    rank = jnp.einsum("met,tu->meu", chosen.astype(BF16), earlier, preferred_element_type=F32)
    micro = jnp.arange(MICRO, dtype=jnp.int32).astype(F32)[:, None, None]
    place = lanes(jnp.where(chosen > 0.5, rank + CAP * micro, -1.0))
    chosen = lanes(chosen)
    places = place[:, None, :]
    route_lanes = jnp.concatenate([routes[0, 0].T, routes[0, 1].T], axis=1)
    picked = (
        route_lanes[:, None, :] == jnp.arange(EXPERTS, dtype=jnp.int32)[None, :, None]
    )

    def norm_scale(values):
        return lax.rsqrt(jnp.mean(values * values, axis=0, keepdims=True) + EPSILON)

    def for_seq(blocks, shared):
        blocks = jnp.transpose(blocks.astype(BF16).reshape(OWN, N_SEQ, -1), (1, 0, 2))
        shared = jnp.concatenate(high_low(shared), axis=1)
        return jnp.concatenate(
            [blocks, jnp.broadcast_to(shared[None], (N_SEQ,) + shared.shape)], axis=2
        )

    def from_seq(blocks, n):
        total = jnp.sum(blocks.astype(F32), axis=0)
        k = (total.shape[1] - n) // 2
        return total[:, :n], total[:, n : n + k] + total[:, n + k :]

    def forward(x_own, x_full, riders):
        x = x_full.astype(F32)
        scale_one = norm_scale(x)
        normed_one = (x * scale_one * gain_one).astype(BF16)
        heads = dot_tn(w_qkv_group, normed_one).reshape(PER_GROUP + 2, HEAD_DIM, TOKENS)
        turned = rotate(heads[: PER_GROUP + 1], cosine, sine)
        turned = jnp.concatenate([turned, heads[PER_GROUP + 1 :]], axis=0).astype(BF16)
        turned = turned.reshape(GROUP_COLS, TOKENS)
        queries = turned[: PER_GROUP * HEAD_DIM]
        sent = jnp.concatenate([turned[PER_GROUP * HEAD_DIM :]] + riders, axis=0)
        key_value = exchange(jnp.broadcast_to(sent[None], (N_SEQ,) + sent.shape), "seq")
        ridden = key_value[:, 2 * HEAD_DIM :]
        key_value = key_value[:, : 2 * HEAD_DIM]
        mixed, log_total = attention_forward(first, queries, key_value)
        mixed_full = rows_of(mixed)
        part, compact, scale_two, logits, gates, middle, normed_two, g, u = experts_forward(
            x_full, mixed_full, gain_two, w_router, chosen, places, w_attn_full, w_in, w_out
        )
        saved = (
            x_own,
            scale_one,
            own(normed_one),
            queries,
            key_value,
            log_total,
            mixed,
            mixed_full,
            middle,
            scale_two,
            normed_two,
            logits,
            gates,
            g,
            u,
        )
        return part.reshape(N_WA, OWN, TOKENS), compact, saved, ridden

    def finish(saved, blocks):
        return (own(saved[8]) + jnp.sum(blocks.astype(F32), axis=0)).astype(BF16)

    def backward(dz, dz_full, saved, alongside, feature, later):
        (
            x_own,
            scale_one,
            own_normed_one,
            queries,
            key_value,
            log_total,
            mixed,
            mixed_full,
            middle,
            scale_two,
            normed_two,
            logits,
            gates,
            g,
            u,
        ) = saved
        blocks, du = experts_backward(
            dz_full, gain_two, gates[:, None, :], places, route_lanes, g, u, middle, w_in, w_out
        )
        blocks, alongside = lax.optimization_barrier((blocks, alongside))
        if later is not None:
            du = of_section(du, later[0])
            blocks, du = lax.optimization_barrier((blocks, du))
        back = exchange(blocks, "wa")
        if later is not None:
            expert_out_grad = weight_grad_out(compact_out, alongside, places_all)
            back, expert_out_grad = lax.optimization_barrier((back, expert_out_grad))
        back = jnp.sum(back.astype(F32), axis=0)
        dgate_top = back[OWN : OWN + TOP]
        inner = back[OWN + TOP : OWN + TOP + 1] + back[OWN + TOP + 1 : OWN + TOP + 2]
        dgate = jnp.sum(jnp.where(picked, dgate_top[:, None, :], 0.0), axis=0)
        dlogit = gates * (dgate - jnp.sum(gates * dgate, axis=0, keepdims=True))
        dlogit_high, dlogit_low = high_low(dlogit)
        own_router = router_weight[0]
        dnormed = back[:OWN] + dot_nn(own_router, dlogit_high) + dot_nn(own_router, dlogit_low)
        inner += jnp.sum(dlogit * logits, axis=0, keepdims=True) / scale_two
        own_middle = own(middle)
        dmiddle = (
            dz.astype(F32)
            + scale_two * own_gain_two * dnormed
            - own_middle * (scale_two * scale_two * scale_two * inner * (1.0 / WIDTH))
        )
        gain_two_grad = jnp.sum(dnormed * own_middle * scale_two, axis=1, keepdims=True)
        own_normed_two = own(normed_two)
        router_grad = dot_nt(own_normed_two, dlogit_high) + dot_nt(own_normed_two, dlogit_low)
        dmiddle_low = dmiddle.astype(BF16)
        attn_grad = dot_nt(dmiddle_low, mixed_full)
        small_grad = jnp.concatenate([gain_two_grad, router_grad], axis=1)
        if later is not None:
            blocks = for_seq(of_section(attn_grad, later[1]), of_section(small_grad, later[2]))
            dmiddle_low, blocks = lax.optimization_barrier((dmiddle_low, blocks))
            attn_grad = exchange(blocks, "seq")
        else:
            dmiddle_low, feature = lax.optimization_barrier((dmiddle_low, feature))
            feature = exchange(feature, "seq")
        dmiddle_full = rows_of(dmiddle_low)
        if later is None:
            dmiddle_full, feature = lax.optimization_barrier((dmiddle_full, feature))
        else:
            dmiddle_full, attn_grad = lax.optimization_barrier((dmiddle_full, attn_grad))
            attn_grad, small_grad = from_seq(attn_grad, OWN)
        dmixed = dot_tn(w_attn_group, dmiddle_full).astype(BF16)
        dq, dkv = attention_backward(first, queries, key_value, mixed, dmixed, log_total)
        dkv = summed(dkv, "seq")
        dturned = jnp.concatenate([dq, dkv], axis=0)
        turned = jnp.concatenate(
            [queries, lax.dynamic_index_in_dim(key_value, s_index, 0, False)], axis=0
        )
        inner_one = jnp.sum(dturned * turned.astype(F32), axis=0, keepdims=True)
        dheads = dturned.reshape(PER_GROUP + 2, HEAD_DIM, TOKENS)
        dheads = jnp.concatenate(
            [rotate(dheads[: PER_GROUP + 1], cosine, -sine), dheads[PER_GROUP + 1 :]], axis=0
        )
        sent = jnp.concatenate(
            [
                dheads.reshape(GROUP_COLS, TOKENS).astype(BF16),
                *high_low(inner_one),
                jnp.zeros((14, TOKENS), BF16),
            ],
            axis=0,
        )
        full = exchange(jnp.broadcast_to(sent[None], (N_WA,) + sent.shape), "wa")
        dheads_full = full[:, :GROUP_COLS].reshape(KV_HEADS * GROUP_COLS, TOKENS)
        inner_one = jnp.sum(
            full[:, GROUP_COLS : GROUP_COLS + 2].astype(F32), axis=(0, 1)
        )[None] / scale_one
        dnormed_one = dot_nn(w_qkv, dheads_full)
        x = x_own.astype(F32)
        dx = (
            dmiddle
            + scale_one * own_gain_one * dnormed_one
            - x * (scale_one * scale_one * scale_one * inner_one * (1.0 / WIDTH))
        )
        gain_one_grad = jnp.sum(dnormed_one * x * scale_one, axis=1, keepdims=True)
        qkv_grad = dot_nt(own_normed_one, dheads_full)
        if later is None:
            return dx, alongside, feature, (du, attn_grad, small_grad, gain_one_grad, qkv_grad)
        blocks = for_seq(of_section(qkv_grad, later[4]), of_section(gain_one_grad, later[3]))
        blocks = exchange(blocks, "seq")
        expert_in_grad = weight_grad_in(
            lax.all_gather(du, "seq", axis=0, tiled=False), feature, places_all
        )
        blocks, expert_in_grad = lax.optimization_barrier((blocks, expert_in_grad))
        qkv_grad, gain_one_grad = from_seq(blocks, GROUP_COLS)
        return (
            dx,
            expert_in_grad,
            expert_out_grad,
            attn_grad,
            small_grad,
            gain_one_grad,
            qkv_grad,
        )

    riders = [jnp.concatenate([place, jnp.zeros((8, TOKENS), F32)], axis=0).astype(BF16)]
    out_one, compact_one, saved_one, ridden = forward(x_first, x_first_full, riders)
    places_all = ridden[:, :EXPERTS].astype(F32)
    places_all = places_all[:, :, None, :]
    out_one = finish(saved_one, exchange(out_one, "wa"))
    received = lax.ppermute(out_one, "section", [(0, 1)])
    out_two, compact_two, saved_two, _ = forward(received, rows_of(received), [])
    out_two = exchange(out_two, "wa")

    feature_in = of_section(saved_one[10], saved_two[10]).reshape(N_SEQ, OWN, TOKENS)
    compact_out = lax.all_gather(of_section(compact_one, compact_two), "seq", axis=0, tiled=False)

    dx_two, out_two, feature_in, later = backward(
        cot, cot_full, saved_two, out_two, feature_in, None
    )
    out_two = finish(saved_two, out_two)
    returned = lax.ppermute(after(dx_two.astype(BF16), compact_out), "section", [(1, 0)])
    returned_full = rows_of(returned)
    feature_out = exchange(
        of_section(returned_full, cot_full).reshape(N_SEQ, OWN, TOKENS), "seq"
    )
    (
        dx_one,
        expert_in_grad,
        expert_out_grad,
        attn_grad,
        small_grad,
        gain_one_grad,
        qkv_grad,
    ) = backward(returned, returned_full, saved_one, feature_out, feature_in, later)

    def tokens_first(values):
        return jnp.transpose(values.reshape(OWN, MICRO, ROWS), (1, 2, 0))[None]

    return (
        tokens_first(of_section(out_one, out_two)),
        tokens_first(of_section(dx_one, dx_two)),
        jnp.stack([gain_one_grad[:, 0], small_grad[:, 0]])[None],
        qkv_grad[None],
        attn_grad[None],
        small_grad[None, :, 1:],
        expert_in_grad.reshape(1, EXPERTS, 2, HIDDEN, OWN),
        expert_out_grad[None],
    )


def solution(mesh):
    return jax.shard_map(
        on_device,
        mesh=mesh,
        in_specs=(
            P(None, "wa", "seq"),
            P("section", None, "seq", None),
            P(None, "wa", "seq"),
            P("section", None, "wa"),
            P("section", "wa", None),
            P("section", "wa", None),
            P("section", "wa", None),
            P("section", None, None, "wa", None),
            P("section", None, "wa", None),
        ),
        out_specs=(
            P("section", None, "seq", "wa"),
            P("section", None, "seq", "wa"),
            P("section", None, "wa"),
            P("section", "wa", "seq"),
            P("section", "wa", "seq"),
            P("section", "wa", None),
            P("section", None, None, "wa", "seq"),
            P("section", None, "wa", "seq"),
        ),
        check_vma=False,
    )
```

```python
import jax
import jax.numpy as jnp
from jax import lax
from jax.experimental import pallas as pl
from jax.experimental.pallas import tpu as pltpu
from jax.sharding import PartitionSpec as P

HEADS = 24
KV_HEADS = 8
PER_GROUP = HEADS // KV_HEADS
HEAD_DIM = 64
EXPERTS = 40
TOP = 8
MICRO = 2
CAP = 32
N_SEQ = 8
N_WA = 8
ROWS = 128
WIDTH = 1536
OWN = WIDTH // N_WA
TOKENS = MICRO * ROWS
LENGTH = ROWS * N_SEQ
HIDDEN = 64
SLOTS = MICRO * CAP
GROUP_COLS = (PER_GROUP + 2) * HEAD_DIM
SENT_COLS = GROUP_COLS + 16
BATCH = 8
STEPS = EXPERTS // BATCH
BLOCK = BATCH * HIDDEN
QUAD = 4
COLUMNS = 256
ATTN_CHUNKS = 4
EXTRA = 16
SCALE = HEAD_DIM ** (-0.5)
EPSILON = 1e-06
BF16 = jnp.bfloat16
F32 = jnp.float32
VMEM_LIMIT = 58 * 1024 * 1024
EXPERT_VMEM = 58 * 1024 * 1024


def dot_nn(a, b):
    return lax.dot_general(a, b, (((1,), (0,)), ((), ())), preferred_element_type=F32)


def dot_nt(a, b):
    return lax.dot_general(a, b, (((1,), (1,)), ((), ())), preferred_element_type=F32)


def dot_tn(a, b):
    return lax.dot_general(a, b, (((0,), (0,)), ((), ())), preferred_element_type=F32)


def params():
    return pltpu.CompilerParams(
        vmem_limit_bytes=VMEM_LIMIT, dimension_semantics=("arbitrary",)
    )


def one_hot_slots(places):
    slot = lax.broadcasted_iota(jnp.int32, (QUAD, SLOTS, TOKENS), 1).astype(F32)
    hit = jnp.where(slot == places, 1.0, 0.0)
    return hit.reshape(QUAD * SLOTS, TOKENS).astype(BF16)


def copied(pairs, sems):
    copies = []
    for k, (source, target) in enumerate(pairs):
        copy = pltpu.make_async_copy(source, target, sems.at[k])
        copy.start()
        copies.append(copy)
    return copies


def chunk_copies(pairs, sems, c):
    copies = []
    for k, (source, target) in enumerate(pairs):
        rows = source.shape[0] // STEPS
        part = pl.ds(pl.multiple_of(c * rows, rows), rows)
        copies.append(pltpu.make_async_copy(source.at[part], target.at[part], sems.at[k, c]))
    return copies


def start_chunks(pairs, sems):
    @pl.loop(0, STEPS)
    def _(c):
        for copy in chunk_copies(pairs, sems, c):
            copy.start()


def accumulate(total, left, right_ref):
    for c in range(0, WIDTH, COLUMNS):
        cols = slice(c, c + COLUMNS)
        total[cols] += dot_tn(right_ref[..., cols].reshape(left.shape[0], COLUMNS), left)


def experts_forward_kernel(
    x_hbm, mixed_hbm, gain_hbm, router_hbm, chosen_hbm, place_hbm, wattn_hbm, win_hbm, wout_hbm,
    y_ref, f_ref, scale_ref, logit_ref, gate_ref, middle_hbm, normed_hbm, g_hbm, u_hbm,
    x_ref, mixed_ref, gain_ref, router_ref, chosen_ref, place_ref, middle_ref, normed_ref,
    gate_rows, wattn, win, wout, g_all, u_all, total, small_sems, attn_sems, in_sems, out_sems,
):
    height = WIDTH // ATTN_CHUNKS
    mixed_copy, x_copy = copied(((mixed_hbm, mixed_ref), (x_hbm, x_ref)), small_sems)
    attn = [
        pltpu.make_async_copy(
            wattn_hbm.at[pl.ds(c * height, height)], wattn.at[pl.ds(c * height, height)], attn_sems.at[c]
        )
        for c in range(ATTN_CHUNKS)
    ]
    for copy in attn:
        copy.start()
    small = copied(
        (
            (gain_hbm, gain_ref),
            (router_hbm, router_ref),
            (chosen_hbm, chosen_ref),
            (place_hbm, place_ref),
        ),
        small_sems.at[pl.ds(2, 4)],
    )
    weights = ((win_hbm, win), (wout_hbm, wout))
    start_chunks(weights, in_sems)
    total[...] = jnp.zeros_like(total)
    mixed_copy.wait()
    x_copy.wait()

    squares = jnp.zeros((1, TOKENS), F32)
    for c in range(ATTN_CHUNKS):
        part = pl.ds(c * height, height)
        attn[c].wait()
        middle = x_ref[part].astype(F32) + dot_nn(wattn[part], mixed_ref[...])
        middle_ref[part] = middle
        squares += jnp.sum(middle * middle, axis=0, keepdims=True)
    scale = lax.rsqrt(squares * (1.0 / WIDTH) + EPSILON)
    scale_ref[...] = scale
    for copy in small:
        copy.wait()
    normed_ref[...] = (middle_ref[...] * scale * gain_ref[...]).astype(BF16)
    logits = dot_tn(router_ref[...], normed_ref[...])
    logit_ref[...] = logits
    chosen = chosen_ref[...] > 0.5
    top = jnp.max(jnp.where(chosen, logits, -1e30), axis=0, keepdims=True)
    raised = jnp.where(chosen, jnp.exp(jnp.where(chosen, logits - top, 0.0)), 0.0)
    gates = raised / jnp.sum(raised, axis=0, keepdims=True)
    gate_ref[...] = gates
    for e in range(EXPERTS):
        gate_rows[e] = gates[e : e + 1]

    leaving = copied(
        ((middle_ref, middle_hbm), (normed_ref, normed_hbm)), small_sems.at[pl.ds(6, 2)]
    )
    lane = lax.broadcasted_iota(jnp.int32, (SLOTS, 2 * HIDDEN), 1)
    hidden = ((g_all, g_hbm), (u_all, u_hbm))

    @pl.loop(0, STEPS)
    def _(c):
        some = pl.ds(c * BATCH, BATCH)
        rows = pl.ds(pl.multiple_of(c * BLOCK, BLOCK), BLOCK)
        win_copy, wout_copy = chunk_copies(weights, in_sems, c)
        win_copy.wait()
        g = dot_nn(win[some, 0].reshape(BLOCK, WIDTH), normed_ref[...])
        u = dot_nn(win[some, 1].reshape(BLOCK, WIDTH), normed_ref[...])
        g_all[rows] = g.astype(BF16)
        u_all[rows] = u.astype(BF16)
        for copy in chunk_copies(hidden, out_sems, c):
            copy.start()
        active = (g * jax.nn.sigmoid(g) * u).astype(BF16).astype(F32)
        gated = (active.reshape(BATCH, HIDDEN, TOKENS) * gate_rows[some]).astype(BF16)
        gated = gated.reshape(BLOCK, TOKENS)
        for q in range(0, BATCH, QUAD):
            pick = one_hot_slots(place_ref[pl.ds(c * BATCH + q, QUAD)])
            every = dot_nt(pick, gated[q * HIDDEN : (q + QUAD) * HIDDEN])
            for p in range(QUAD // 2):
                lanes = slice(2 * p * HIDDEN, 2 * (p + 1) * HIDDEN)
                even = every[2 * p * SLOTS : (2 * p + 1) * SLOTS, lanes]
                odd = every[(2 * p + 1) * SLOTS : (2 * p + 2) * SLOTS, lanes]
                row = pl.multiple_of((c * BATCH + q) // 2 * SLOTS + p * SLOTS, SLOTS)
                f_ref[pl.ds(row, SLOTS)] = jnp.where(lane < HIDDEN, even, odd).astype(BF16)
        wout_copy.wait()
        accumulate(total, gated, wout.at[some])

    y_ref[...] = total[...].astype(BF16)
    for copy in leaving:
        copy.wait()

    @pl.loop(0, STEPS)
    def _(c):
        for copy in chunk_copies(hidden, out_sems, c):
            copy.wait()


def vmem_spec():
    return pl.BlockSpec(memory_space=pltpu.VMEM)


def any_spec():
    return pl.BlockSpec(memory_space=pl.ANY)


def expert_scratch():
    return [
        pltpu.VMEM((EXPERTS, 2, HIDDEN, WIDTH), BF16),
        pltpu.VMEM((EXPERTS, HIDDEN, WIDTH), BF16),
        pltpu.VMEM((EXPERTS * HIDDEN, TOKENS), BF16),
        pltpu.VMEM((EXPERTS * HIDDEN, TOKENS), BF16),
        pltpu.VMEM((WIDTH, TOKENS), F32),
    ]


def expert_cost():
    return pl.CostEstimate(
        flops=6 * TOKENS * EXPERTS * HIDDEN * WIDTH, bytes_accessed=28_000_000, transcendentals=0
    )


def experts_forward(x, mixed, gain, router, chosen, places, w_attn, w_in, w_out):
    hidden = jax.ShapeDtypeStruct((EXPERTS * HIDDEN, TOKENS), BF16)
    some = jax.ShapeDtypeStruct((EXPERTS, TOKENS), F32)
    return pl.pallas_call(
        experts_forward_kernel,
        in_specs=[any_spec()] * 9,
        out_specs=[vmem_spec()] * 5 + [any_spec()] * 4,
        out_shape=[
            jax.ShapeDtypeStruct((WIDTH, TOKENS), BF16),
            jax.ShapeDtypeStruct((EXPERTS // 2 * SLOTS, 2 * HIDDEN), BF16),
            jax.ShapeDtypeStruct((1, TOKENS), F32),
            some,
            some,
            jax.ShapeDtypeStruct((WIDTH, TOKENS), F32),
            jax.ShapeDtypeStruct((WIDTH, TOKENS), BF16),
            hidden,
            hidden,
        ],
        scratch_shapes=[
            pltpu.VMEM((WIDTH, TOKENS), BF16),
            pltpu.VMEM((WIDTH, TOKENS), BF16),
            pltpu.VMEM((WIDTH, 1), F32),
            pltpu.VMEM((WIDTH, EXPERTS), BF16),
            pltpu.VMEM((EXPERTS, TOKENS), F32),
            pltpu.VMEM((EXPERTS, 1, TOKENS), F32),
            pltpu.VMEM((WIDTH, TOKENS), F32),
            pltpu.VMEM((WIDTH, TOKENS), BF16),
            pltpu.VMEM((EXPERTS, 1, TOKENS), F32),
            pltpu.VMEM((WIDTH, WIDTH), BF16),
        ]
        + expert_scratch()
        + [pltpu.SemaphoreType.DMA((8,)), pltpu.SemaphoreType.DMA((ATTN_CHUNKS,))]
        + [pltpu.SemaphoreType.DMA((2, STEPS))] * 2,
        compiler_params=pltpu.CompilerParams(vmem_limit_bytes=EXPERT_VMEM),
        cost_estimate=expert_cost(),
        name="experts_forward",
    )(x, mixed, gain, router, chosen, places, w_attn, w_in, w_out)


def experts_backward_kernel(
    dz_hbm, gain_hbm, gate_hbm, place_hbm, route_hbm,
    g_hbm, u_hbm, middle_hbm, win_hbm, wout_hbm,
    out_ref, du_ref,
    dz_ref, gain_ref, gate_ref, place_ref, route_ref,
    win, wout, g_all, u_all, total, middle_all, dgate_all, in_sems, small_sems,
):
    dz_copy, gate_copy, place_copy = copied(
        ((dz_hbm, dz_ref), (gate_hbm, gate_ref), (place_hbm, place_ref)), small_sems
    )
    pairs = ((wout_hbm, wout), (g_hbm, g_all), (u_hbm, u_all), (win_hbm, win))
    start_chunks(pairs, in_sems)
    total[...] = jnp.zeros_like(total)
    late = copied(
        ((middle_hbm, middle_all), (gain_hbm, gain_ref), (route_hbm, route_ref)),
        small_sems.at[pl.ds(3, 3)],
    )
    dz_copy.wait()
    gate_copy.wait()
    place_copy.wait()

    @pl.loop(0, STEPS)
    def _(c):
        some = pl.ds(c * BATCH, BATCH)
        rows = pl.ds(pl.multiple_of(c * BLOCK, BLOCK), BLOCK)
        wout_copy, g_copy, u_copy, win_copy = chunk_copies(pairs, in_sems, c)
        wout_copy.wait()
        through = dot_nn(wout[some].reshape(BLOCK, WIDTH), dz_ref[...])
        g_copy.wait()
        u_copy.wait()
        g = g_all[rows].astype(F32)
        u = u_all[rows].astype(F32)
        sig = jax.nn.sigmoid(g)
        silu = g * sig
        active = (silu * u).astype(BF16).astype(F32)
        dgate_all[pl.ds(pl.multiple_of(c * BATCH, BATCH), BATCH)] = jnp.sum(
            (active * through).reshape(BATCH, HIDDEN, TOKENS), axis=1
        )
        df = (through.reshape(BATCH, HIDDEN, TOKENS) * gate_ref[some]).reshape(BLOCK, TOKENS)
        dg = (df * u * (sig * (1.0 + g * (1.0 - sig)))).astype(BF16)
        du = (df * silu).astype(BF16)
        both = jnp.concatenate(
            [dg.reshape(BATCH, 1, HIDDEN, TOKENS), du.reshape(BATCH, 1, HIDDEN, TOKENS)], axis=1
        ).reshape(2 * BLOCK, TOKENS)
        for q in range(0, BATCH, QUAD):
            pick = one_hot_slots(place_ref[pl.ds(c * BATCH + q, QUAD)])
            every = dot_nt(pick, both[2 * q * HIDDEN : 2 * (q + QUAD) * HIDDEN])
            for e in range(QUAD):
                row = pl.multiple_of((c * BATCH + q + e) * SLOTS, SLOTS)
                du_ref[pl.ds(row, SLOTS)] = every[
                    e * SLOTS : (e + 1) * SLOTS, 2 * e * HIDDEN : 2 * (e + 1) * HIDDEN
                ].astype(BF16)
        win_copy.wait()
        accumulate(total, both, win.at[some])

    for copy in late:
        copy.wait()
    inner = jnp.zeros((1, TOKENS), F32)
    for w in range(N_WA):
        part = pl.ds(w * OWN, OWN)
        share = total[part].astype(BF16)
        out_ref[w, :OWN] = share
        inner += jnp.sum(
            share.astype(F32) * middle_all[part] * gain_ref[part], axis=0, keepdims=True
        )
    expert = lax.broadcasted_iota(jnp.int32, (EXPERTS, TOKENS), 0)
    dgate = dgate_all[...]
    tops = [
        jnp.sum(jnp.where(expert == route_ref[k : k + 1], dgate, 0.0), axis=0, keepdims=True)
        for k in range(TOP)
    ]
    high = inner.astype(BF16).astype(F32)
    extra = jnp.concatenate(
        tops + [high, inner - high, jnp.zeros((EXTRA - TOP - 2, TOKENS), F32)], axis=0
    ).astype(BF16)
    for w in range(N_WA):
        out_ref[w, OWN:] = extra


def experts_backward(dz, gain, gates, places, routes, g, u, middle, w_in, w_out):
    return pl.pallas_call(
        experts_backward_kernel,
        in_specs=[any_spec()] * 10,
        out_specs=[vmem_spec()] * 2,
        out_shape=[
            jax.ShapeDtypeStruct((N_WA, OWN + EXTRA, TOKENS), BF16),
            jax.ShapeDtypeStruct((EXPERTS * SLOTS, 2 * HIDDEN), BF16),
        ],
        scratch_shapes=[
            pltpu.VMEM((WIDTH, TOKENS), BF16),
            pltpu.VMEM((WIDTH, 1), F32),
            pltpu.VMEM((EXPERTS, 1, TOKENS), F32),
            pltpu.VMEM((EXPERTS, 1, TOKENS), F32),
            pltpu.VMEM((TOP, TOKENS), jnp.int32),
        ]
        + expert_scratch()
        + [
            pltpu.VMEM((WIDTH, TOKENS), F32),
            pltpu.VMEM((EXPERTS, TOKENS), F32),
            pltpu.SemaphoreType.DMA((4, STEPS)),
            pltpu.SemaphoreType.DMA((6,)),
        ],
        compiler_params=pltpu.CompilerParams(vmem_limit_bytes=EXPERT_VMEM),
        cost_estimate=expert_cost(),
        name="experts_backward",
    )(dz, gain, gates, places, routes, g, u, middle, w_in, w_out)


def slot_rows(feature_ref, place_ref):
    rows = []
    for s in range(N_SEQ):
        rows.append(dot_nt(one_hot_slots(place_ref[s]), feature_ref[s]).astype(BF16))
    return [
        jnp.concatenate([r[e * SLOTS : (e + 1) * SLOTS] for r in rows], axis=0)
        for e in range(QUAD)
    ]


def weight_grad_in_kernel(compact_ref, feature_ref, place_ref, out_ref):
    rows = slot_rows(feature_ref, place_ref)
    for e in range(QUAD):
        left = jnp.concatenate(
            [compact_ref[s, e * SLOTS : (e + 1) * SLOTS] for s in range(N_SEQ)], axis=0
        )
        out_ref[e] = dot_tn(left, rows[e])


def weight_grad_out_kernel(compact_ref, feature_ref, place_ref, out_ref):
    rows = slot_rows(feature_ref, place_ref)
    for p in range(QUAD // 2):
        left = jnp.concatenate(
            [compact_ref[s, p * SLOTS : (p + 1) * SLOTS] for s in range(N_SEQ)], axis=0
        )
        out_ref[2 * p] = dot_tn(left, rows[2 * p])[:HIDDEN]
        out_ref[2 * p + 1] = dot_tn(left, rows[2 * p + 1])[HIDDEN:]


def weight_grad(kernel, compact, feature, places, height):
    block = compact.shape[1] * QUAD // EXPERTS
    return pl.pallas_call(
        kernel,
        grid=(EXPERTS // QUAD,),
        in_specs=[
            pl.BlockSpec((N_SEQ, block, 2 * HIDDEN), lambda i: (0, i, 0)),
            pl.BlockSpec((N_SEQ, OWN, TOKENS), lambda i: (0, 0, 0)),
            pl.BlockSpec((N_SEQ, QUAD, 1, TOKENS), lambda i: (0, i, 0, 0)),
        ],
        out_specs=pl.BlockSpec((QUAD, height, OWN), lambda i: (i, 0, 0)),
        out_shape=jax.ShapeDtypeStruct((EXPERTS, height, OWN), F32),
        compiler_params=params(),
        cost_estimate=pl.CostEstimate(
            flops=2 * N_SEQ * TOKENS * EXPERTS * SLOTS * OWN, bytes_accessed=15_000_000, transcendentals=0
        ),
        name="expert_weight_grad",
    )(compact, feature, places)


def weight_grad_in(compact, feature, places):
    return weight_grad(weight_grad_in_kernel, compact, feature, places, 2 * HIDDEN)


def weight_grad_out(compact, feature, places):
    return weight_grad(weight_grad_out_kernel, compact, feature, places, HIDDEN)


def causal_mask(first):
    key = lax.broadcasted_iota(jnp.int32, (LENGTH, ROWS), 0)
    query = lax.broadcasted_iota(jnp.int32, (LENGTH, ROWS), 1) + first
    return key <= query


def side_by_side(parts):
    return jnp.concatenate(parts, axis=1)


def attention_forward_kernel(first_ref, q_ref, kv_ref, o_ref, lse_ref):
    keys = side_by_side([kv_ref[s, :HEAD_DIM] for s in range(N_SEQ)])
    values = side_by_side([kv_ref[s, HEAD_DIM:] for s in range(N_SEQ)])
    keep = causal_mask(first_ref[0])
    for h in range(PER_GROUP):
        rows = slice(h * HEAD_DIM, (h + 1) * HEAD_DIM)
        scores = jnp.where(keep, dot_tn(keys, q_ref[rows]) * SCALE, -1e30)
        top = jnp.max(scores, axis=0, keepdims=True)
        raised = jnp.exp(scores - top)
        total = jnp.sum(raised, axis=0, keepdims=True)
        probs = (raised * (1.0 / total)).astype(BF16)
        o_ref[rows] = dot_nn(values, probs).astype(BF16)
        lse_ref[h] = top + jnp.log(total)


def attention_forward(first, q, kv):
    return pl.pallas_call(
        attention_forward_kernel,
        grid=(MICRO,),
        in_specs=[
            pl.BlockSpec(memory_space=pltpu.SMEM),
            pl.BlockSpec((PER_GROUP * HEAD_DIM, ROWS), lambda m: (0, m)),
            pl.BlockSpec((N_SEQ, 2 * HEAD_DIM, ROWS), lambda m: (0, 0, m)),
        ],
        out_specs=[
            pl.BlockSpec((PER_GROUP * HEAD_DIM, ROWS), lambda m: (0, m)),
            pl.BlockSpec((PER_GROUP, 1, ROWS), lambda m: (0, 0, m)),
        ],
        out_shape=[
            jax.ShapeDtypeStruct((PER_GROUP * HEAD_DIM, TOKENS), BF16),
            jax.ShapeDtypeStruct((PER_GROUP, 1, TOKENS), F32),
        ],
        compiler_params=params(),
        name="attention_forward",
    )(first, q, kv)


def attention_backward_kernel(first_ref, q_ref, kv_ref, o_ref, do_ref, lse_ref, dq_ref, dkv_ref):
    keys = side_by_side([kv_ref[s, :HEAD_DIM] for s in range(N_SEQ)])
    values = side_by_side([kv_ref[s, HEAD_DIM:] for s in range(N_SEQ)])
    keep = causal_mask(first_ref[0])
    dkeys = jnp.zeros((HEAD_DIM, LENGTH), F32)
    dvalues = jnp.zeros((HEAD_DIM, LENGTH), F32)
    for h in range(PER_GROUP):
        rows = slice(h * HEAD_DIM, (h + 1) * HEAD_DIM)
        query = q_ref[rows]
        dout = do_ref[rows]
        scores = jnp.where(keep, dot_tn(keys, query) * SCALE, -1e30)
        probs = jnp.exp(scores - lse_ref[h])
        dvalues += dot_nt(dout, probs.astype(BF16))
        inner = jnp.sum(
            dout.astype(F32) * o_ref[rows].astype(F32), axis=0, keepdims=True
        )
        dscores = (probs * (dot_tn(values, dout) - inner)).astype(BF16)
        dkeys += dot_nt(query, dscores)
        dq_ref[rows] = dot_nn(keys, dscores) * SCALE
    dkeys = (dkeys * SCALE).astype(BF16)
    dvalues = dvalues.astype(BF16)
    for s in range(N_SEQ):
        lanes = slice(s * ROWS, (s + 1) * ROWS)
        dkv_ref[s, :HEAD_DIM] = dkeys[:, lanes]
        dkv_ref[s, HEAD_DIM:] = dvalues[:, lanes]


def attention_backward(first, q, kv, o, do, lse):
    q_spec = pl.BlockSpec((PER_GROUP * HEAD_DIM, ROWS), lambda m: (0, m))
    kv_spec = pl.BlockSpec((N_SEQ, 2 * HEAD_DIM, ROWS), lambda m: (0, 0, m))
    return pl.pallas_call(
        attention_backward_kernel,
        grid=(MICRO,),
        in_specs=[
            pl.BlockSpec(memory_space=pltpu.SMEM),
            q_spec,
            kv_spec,
            q_spec,
            q_spec,
            pl.BlockSpec((PER_GROUP, 1, ROWS), lambda m: (0, 0, m)),
        ],
        out_specs=[q_spec, kv_spec],
        out_shape=[
            jax.ShapeDtypeStruct((PER_GROUP * HEAD_DIM, TOKENS), F32),
            jax.ShapeDtypeStruct((N_SEQ, 2 * HEAD_DIM, TOKENS), BF16),
        ],
        compiler_params=params(),
        name="attention_backward",
    )(first, q, kv, o, do, lse)


def rotate(values, cosine, sine):
    half = HEAD_DIM // 2
    a, b = values[:, :half], values[:, half:]
    return jnp.concatenate([a * cosine - b * sine, b * cosine + a * sine], axis=1)


def high_low(values):
    high = lax.reduce_precision(values, 8, 7)
    return high.astype(BF16), (values - high).astype(BF16)


def after(value, *others):
    return lax.optimization_barrier((value,) + others)[0]


def exchange(blocks, axis):
    return lax.all_to_all(blocks, axis, split_axis=0, concat_axis=0, tiled=False)


def summed(blocks, axis):
    return jnp.sum(exchange(blocks, axis).astype(F32), axis=0)


def on_device(
    first_layer_input,
    routes,
    cotangent,
    gains,
    qkv_weight,
    out_weight,
    router_weight,
    expert_in,
    expert_out,
):
    section_first = lax.axis_index("section") == 0
    s_index = lax.axis_index("seq")
    w_index = lax.axis_index("wa")
    first = jnp.reshape(s_index * ROWS, (1,)).astype(jnp.int32)

    def rows_of(values):
        return lax.all_gather(values, "wa", axis=0, tiled=True)

    def own(values):
        return lax.dynamic_slice_in_dim(values, w_index * OWN, OWN, 0)

    def lanes(values):
        return jnp.concatenate([values[0], values[1]], axis=1)

    def reduced(blocks):
        pairs = blocks.reshape((chips, 2) + blocks.shape[1:])
        kept = lax.dynamic_index_in_dim(pairs, core, 1, False).astype(F32)
        sent = lax.dynamic_index_in_dim(pairs, 1 - core, 1, False)
        kept += lax.ppermute(sent, "wa", [(i, i ^ 1) for i in range(N_WA)]).astype(F32)
        total = lax.dynamic_index_in_dim(kept, chip, 0, False)
        kept = kept.astype(BF16)
        for d in (1, chips - 1, 2):
            route = [(i, (i // 2 + d) % chips * 2 + i % 2) for i in range(N_WA)]
            sent = lax.dynamic_index_in_dim(kept, (chip + d) % chips, 0, False)
            total += lax.ppermute(sent, "wa", route).astype(F32)
        return total

    core, chip, chips = w_index % 2, w_index // 2, N_WA // 2

    def gathered(block):
        arrived = []
        for d in (chips - 1, 2, 1):
            route = [(i, (i // 2 + d) % chips * 2 + i % 2) for i in range(N_WA)]
            arrived.append(lax.ppermute(block, "wa", route))
        mine = jnp.concatenate(arrived + [block], axis=0)
        return mine, lax.ppermute(mine, "wa", [(i, i ^ 1) for i in range(N_WA)])

    def to_arrival(columns):
        parts = columns.reshape(columns.shape[0], chips, 2, -1)
        parts = lax.dynamic_slice_in_dim(
            jnp.concatenate([parts, parts], axis=1), chip + 1, chips, 1
        )
        return lax.optimization_barrier(
            tuple(
                lax.dynamic_index_in_dim(parts, c, 2, False).reshape(columns.shape[0], -1)
                for c in (core, 1 - core)
            )
        )

    def from_arrival(halves):
        mine, other = (
            lax.dynamic_slice_in_dim(
                jnp.concatenate([half.reshape(half.shape[0], chips, -1)] * 2, axis=1),
                chips - 1 - chip,
                chips,
                1,
            )
            for half in halves
        )
        pairs = [jnp.where(core == 0, mine, other), jnp.where(core == 0, other, mine)]
        return jnp.stack(pairs, axis=2).reshape(mine.shape[0], -1)

    def of_section(one, two):
        return jnp.where(section_first, one, two)

    x_first = lanes(first_layer_input)
    cot = lanes(cotangent)
    gain_pair = gains[0].T
    gain_high = lax.reduce_precision(gain_pair, 8, 7)
    gain_rest, gain_low = high_low(gain_pair - gain_high)
    gain_high = gain_high.astype(BF16)
    w_qkv = qkv_weight[0]
    w_qkv_blocks = jnp.transpose(w_qkv.reshape(OWN, KV_HEADS, GROUP_COLS), (1, 0, 2))
    packed = jnp.concatenate([x_first, router_weight[0], gain_high, gain_rest, gain_low], axis=1)
    packed, w_qkv_blocks = lax.optimization_barrier((packed, w_qkv_blocks))
    w_qkv_group = exchange(w_qkv_blocks, "wa").reshape(WIDTH, GROUP_COLS)
    packed = rows_of(packed)
    x_first_full = packed[:, :TOKENS]
    w_router = packed[:, TOKENS : TOKENS + EXPERTS]
    gain_parts = packed[:, TOKENS + EXPERTS :].astype(F32)
    gain_parts = gain_parts[:, 0:2] + gain_parts[:, 2:4] + gain_parts[:, 4:6]
    gain_one, gain_two = gain_parts[:, 0:1], gain_parts[:, 1:2]
    w_qkv_wide = to_arrival(
        jnp.pad(
            w_qkv.reshape(OWN, KV_HEADS, GROUP_COLS),
            ((0, 0), (0, 0), (0, SENT_COLS - GROUP_COLS)),
        ).reshape(OWN, KV_HEADS * SENT_COLS)
    )
    w_attn_full = rows_of(after(out_weight[0], packed, w_qkv_group))
    w_attn_group = to_arrival(lax.dynamic_slice_in_dim(w_attn_full, w_index * OWN, OWN, 1).T)
    cot_full = rows_of(cot)
    w_in = expert_in[0]
    w_out = expert_out[0]
    own_gain_one = gains[0, 0][:, None]
    own_gain_two = gains[0, 1][:, None]

    position = (s_index * ROWS + jnp.arange(ROWS, dtype=jnp.int32)).astype(F32)
    frequency = 10000.0 ** (
        -jnp.arange(HEAD_DIM // 2).astype(F32) * (2.0 / HEAD_DIM)
    )
    angle = frequency[:, None] * position[None, :]
    cosine = jnp.tile(jnp.cos(angle), (1, MICRO))
    sine = jnp.tile(jnp.sin(angle), (1, MICRO))

    experts = jnp.arange(EXPERTS, dtype=jnp.int32)[None, :, None]
    chosen = jnp.zeros((MICRO, EXPERTS, ROWS), F32)
    for k in range(TOP):
        chosen += (routes[0][:, None, :, k] == experts).astype(F32)
    earlier = jnp.triu(jnp.ones((ROWS, ROWS), BF16), 1)
    rank = jnp.einsum("met,tu->meu", chosen.astype(BF16), earlier, preferred_element_type=F32)
    micro = jnp.arange(MICRO, dtype=jnp.int32).astype(F32)[:, None, None]
    place = lanes(jnp.where(chosen > 0.5, rank + CAP * micro, -1.0))
    chosen = lanes(chosen)
    places = place[:, None, :]
    route_lanes = jnp.concatenate([routes[0, 0].T, routes[0, 1].T], axis=1)
    picked = (
        route_lanes[:, None, :] == jnp.arange(EXPERTS, dtype=jnp.int32)[None, :, None]
    )

    def norm_scale(values):
        return lax.rsqrt(jnp.mean(values * values, axis=0, keepdims=True) + EPSILON)

    def for_seq(parts, shared):
        blocks = jnp.concatenate(
            [
                jnp.transpose(part.astype(BF16).reshape(OWN, N_SEQ, -1), (1, 0, 2))
                for part in parts
            ],
            axis=2,
        )
        shared = jnp.concatenate(high_low(shared), axis=1)
        return jnp.concatenate(
            [blocks, jnp.broadcast_to(shared[None], (N_SEQ,) + shared.shape)], axis=2
        )

    def from_seq(blocks, n):
        total = jnp.sum(blocks.astype(F32), axis=0)
        k = (total.shape[1] - n) // 2
        return total[:, :n], total[:, n : n + k] + total[:, n + k :]

    def forward(x_own, x_full):
        x = x_full.astype(F32)
        scale_one = norm_scale(x)
        normed_one = (x * scale_one * gain_one).astype(BF16)
        heads = dot_tn(w_qkv_group, normed_one).reshape(PER_GROUP + 2, HEAD_DIM, TOKENS)
        turned = rotate(heads[: PER_GROUP + 1], cosine, sine)
        turned = jnp.concatenate([turned, heads[PER_GROUP + 1 :]], axis=0).astype(BF16)
        turned = turned.reshape(GROUP_COLS, TOKENS)
        queries = turned[: PER_GROUP * HEAD_DIM]
        sent = turned[PER_GROUP * HEAD_DIM :]
        key_value = exchange(jnp.broadcast_to(sent[None], (N_SEQ,) + sent.shape), "seq")
        mixed, log_total = attention_forward(first, queries, key_value)
        mixed_full = rows_of(mixed)
        part, compact, scale_two, logits, gates, middle, normed_two, g, u = experts_forward(
            x_full, mixed_full, gain_two, w_router, chosen, places, w_attn_full, w_in, w_out
        )
        saved = (
            x_own,
            scale_one,
            own(normed_one),
            queries,
            key_value,
            log_total,
            mixed,
            mixed_full,
            middle,
            scale_two,
            normed_two,
            logits,
            gates,
            g,
            u,
        )
        return part.reshape(N_WA, OWN, TOKENS), compact, saved

    def finish(saved, total):
        return (own(saved[8]) + total).astype(BF16)

    def backward(dz, dz_full, saved, alongside, feature, later):
        (
            x_own,
            scale_one,
            own_normed_one,
            queries,
            key_value,
            log_total,
            mixed,
            mixed_full,
            middle,
            scale_two,
            normed_two,
            logits,
            gates,
            g,
            u,
        ) = saved
        blocks, du = experts_backward(
            dz_full, gain_two, gates[:, None, :], places, route_lanes, g, u, middle, w_in, w_out
        )
        blocks, alongside = lax.optimization_barrier((blocks, alongside))
        back = reduced(blocks)
        if later is not None:
            du = of_section(du, later[0])
            back, du = lax.optimization_barrier((back, du))
        dgate_top = back[OWN : OWN + TOP]
        inner = back[OWN + TOP : OWN + TOP + 1] + back[OWN + TOP + 1 : OWN + TOP + 2]
        dgate = jnp.sum(jnp.where(picked, dgate_top[:, None, :], 0.0), axis=0)
        dlogit = gates * (dgate - jnp.sum(gates * dgate, axis=0, keepdims=True))
        dlogit_low = dlogit.astype(BF16)
        dnormed = back[:OWN] + dot_nn(router_weight[0], dlogit_low)
        inner += jnp.sum(dlogit * logits, axis=0, keepdims=True) / scale_two
        own_middle = own(middle)
        dmiddle = (
            dz.astype(F32)
            + scale_two * own_gain_two * dnormed
            - own_middle * (scale_two * scale_two * scale_two * inner * (1.0 / WIDTH))
        )
        gain_two_grad = jnp.sum(dnormed * own_middle * scale_two, axis=1, keepdims=True)
        own_normed_two = own(normed_two)
        router_grad = dot_nt(own_normed_two, dlogit_low)
        dmiddle_low = dmiddle.astype(BF16)
        attn_grad = dot_nt(dmiddle_low, mixed_full)
        small_grad = jnp.concatenate([gain_two_grad, router_grad], axis=1)
        if later is None:
            dmiddle_low, feature = lax.optimization_barrier((dmiddle_low, feature))
            feature = exchange(feature, "seq")
        dmiddle_full = gathered(dmiddle_low)
        if later is None:
            dmiddle_full, feature = lax.optimization_barrier((dmiddle_full, feature))
        dmixed = sum(dot_nn(w, d) for w, d in zip(w_attn_group, dmiddle_full)).astype(BF16)
        dq, dkv = attention_backward(first, queries, key_value, mixed, dmixed, log_total)
        dkv = summed(dkv, "seq")
        dturned = jnp.concatenate([dq, dkv], axis=0)
        turned = jnp.concatenate(
            [queries, lax.dynamic_index_in_dim(key_value, s_index, 0, False)], axis=0
        )
        inner_one = jnp.sum(dturned * turned.astype(F32), axis=0, keepdims=True)
        dheads = dturned.reshape(PER_GROUP + 2, HEAD_DIM, TOKENS)
        dheads = jnp.concatenate(
            [rotate(dheads[: PER_GROUP + 1], cosine, -sine), dheads[PER_GROUP + 1 :]], axis=0
        )
        sent = jnp.concatenate(
            [
                dheads.reshape(GROUP_COLS, TOKENS).astype(BF16),
                *high_low(inner_one),
                jnp.zeros((14, TOKENS), BF16),
            ],
            axis=0,
        )
        full = gathered(sent)
        if later is not None:
            expert_out_grad = weight_grad_out(alongside[1], alongside[0], places_all)
            attn_grad, small_grad = jax.tree.map(of_section, (attn_grad, small_grad), later[1:3])
            blocks = exchange(for_seq((attn_grad,), small_grad), "seq")
            full, expert_out_grad, blocks = lax.optimization_barrier(
                (full, expert_out_grad, blocks)
            )
            attn_grad, small_grad = from_seq(blocks, OWN)
        inner_one = jnp.sum(
            jnp.stack([half.reshape(chips, SENT_COLS, TOKENS) for half in full])[
                :, :, GROUP_COLS : GROUP_COLS + 2
            ].astype(F32),
            axis=(0, 1, 2),
        )[None] / scale_one
        dnormed_one = sum(dot_nn(w, d) for w, d in zip(w_qkv_wide, full))
        x = x_own.astype(F32)
        dx = (
            dmiddle
            + scale_one * own_gain_one * dnormed_one
            - x * (scale_one * scale_one * scale_one * inner_one * (1.0 / WIDTH))
        )
        gain_one_grad = jnp.sum(dnormed_one * x * scale_one, axis=1, keepdims=True)
        qkv_grad = tuple(dot_nt(own_normed_one, half).astype(BF16) for half in full)
        if later is None:
            return dx, alongside, feature, (du, attn_grad, small_grad, gain_one_grad, qkv_grad)
        gain_one_grad, qkv_grad = jax.tree.map(of_section, (gain_one_grad, qkv_grad), later[3:])
        blocks = exchange(for_seq((from_arrival(qkv_grad),), gain_one_grad), "seq")
        expert_in_grad = weight_grad_in(
            lax.all_gather(du, "seq", axis=0, tiled=False), feature, places_all
        )
        blocks, expert_in_grad = lax.optimization_barrier((blocks, expert_in_grad))
        qkv_grad, gain_one_grad = from_seq(blocks, SENT_COLS)
        small_grad = jnp.concatenate([gain_one_grad, small_grad], axis=1)
        return dx, expert_in_grad, expert_out_grad, attn_grad, qkv_grad, small_grad

    out_one, compact_one, saved_one = forward(x_first, x_first_full)
    out_one = finish(saved_one, reduced(out_one))
    received = lax.ppermute(out_one, "section", [(0, 1)])
    out_two, compact_two, saved_two = forward(received, rows_of(received))
    out_two = exchange(out_two, "wa")

    feature_in = of_section(saved_one[10], saved_two[10]).reshape(N_SEQ, OWN, TOKENS)
    riders = jnp.concatenate([place, jnp.zeros((8, TOKENS), F32)], axis=0).astype(BF16)
    feature_in = jnp.concatenate(
        [feature_in, jnp.broadcast_to(riders[None], (N_SEQ,) + riders.shape)], axis=1
    )
    compact_out = lax.all_gather(of_section(compact_one, compact_two), "seq", axis=0, tiled=False)

    dx_two, out_two, feature_in, later = backward(
        cot, cot_full, saved_two, out_two, feature_in, None
    )
    places_all = feature_in[:, OWN : OWN + EXPERTS].astype(F32)[:, :, None, :]
    out_two = finish(saved_two, jnp.sum(out_two.astype(F32), axis=0))
    returned = lax.ppermute(dx_two.astype(BF16), "section", [(1, 0)])
    returned_full = rows_of(returned)
    feature_out = exchange(
        of_section(returned_full, cot_full).reshape(N_SEQ, OWN, TOKENS), "seq"
    )
    dx_one, expert_in_grad, expert_out_grad, attn_grad, qkv_grad, small_grad = backward(
        returned, returned_full, saved_one, (feature_out, compact_out), feature_in, later
    )

    def tokens_first(values):
        return jnp.transpose(values.reshape(OWN, MICRO, ROWS), (1, 2, 0))[None]

    return (
        tokens_first(of_section(out_one, out_two)),
        tokens_first(of_section(dx_one, dx_two)),
        small_grad[:, :2].T[None],
        qkv_grad[None, :, :GROUP_COLS],
        attn_grad[None],
        small_grad[None, :, 2:],
        expert_in_grad.reshape(1, EXPERTS, 2, HIDDEN, OWN),
        expert_out_grad[None],
    )


def solution(mesh):
    return jax.shard_map(
        on_device,
        mesh=mesh,
        in_specs=(
            P(None, "wa", "seq"),
            P("section", None, "seq", None),
            P(None, "wa", "seq"),
            P("section", None, "wa"),
            P("section", "wa", None),
            P("section", "wa", None),
            P("section", "wa", None),
            P("section", None, None, "wa", None),
            P("section", None, "wa", None),
        ),
        out_specs=(
            P("section", None, "seq", "wa"),
            P("section", None, "seq", "wa"),
            P("section", None, "wa"),
            P("section", "wa", "seq"),
            P("section", "wa", "seq"),
            P("section", "wa", None),
            P("section", None, None, "wa", "seq"),
            P("section", None, "wa", "seq"),
        ),
        check_vma=False,
    )
```

```python
import jax
import jax.numpy as jnp
from jax import lax
from jax.experimental import pallas as pl
from jax.experimental.pallas import tpu as pltpu
from jax.sharding import PartitionSpec as P

HEADS = 24
KV_HEADS = 8
PER_GROUP = HEADS // KV_HEADS
HEAD_DIM = 64
EXPERTS = 40
TOP = 8
MICRO = 2
CAP = 32
N_SEQ = 8
N_WA = 8
ROWS = 128
WIDTH = 1536
OWN = WIDTH // N_WA
TOKENS = MICRO * ROWS
LENGTH = ROWS * N_SEQ
HIDDEN = 64
SLOTS = MICRO * CAP
GROUP_COLS = (PER_GROUP + 2) * HEAD_DIM
SENT_COLS = GROUP_COLS + 16
BATCH = 8
STEPS = EXPERTS // BATCH
BLOCK = BATCH * HIDDEN
QUAD = 4
COLUMNS = 256
ATTN_CHUNKS = 4
EXTRA = 16
SCALE = HEAD_DIM ** (-0.5)
EPSILON = 1e-06
BF16 = jnp.bfloat16
F32 = jnp.float32
VMEM_LIMIT = 58 * 1024 * 1024
EXPERT_VMEM = 58 * 1024 * 1024


def dot_nn(a, b):
    return lax.dot_general(a, b, (((1,), (0,)), ((), ())), preferred_element_type=F32)


def dot_nt(a, b):
    return lax.dot_general(a, b, (((1,), (1,)), ((), ())), preferred_element_type=F32)


def dot_tn(a, b):
    return lax.dot_general(a, b, (((0,), (0,)), ((), ())), preferred_element_type=F32)


def params():
    return pltpu.CompilerParams(
        vmem_limit_bytes=VMEM_LIMIT, dimension_semantics=("arbitrary",)
    )


def one_hot_slots(places):
    slot = lax.broadcasted_iota(jnp.int32, (QUAD, SLOTS, TOKENS), 1).astype(F32)
    hit = jnp.where(slot == places, 1.0, 0.0)
    return hit.reshape(QUAD * SLOTS, TOKENS).astype(BF16)


def copied(pairs, sems):
    copies = []
    for k, (source, target) in enumerate(pairs):
        copy = pltpu.make_async_copy(source, target, sems.at[k])
        copy.start()
        copies.append(copy)
    return copies


def chunk_copies(pairs, sems, c):
    copies = []
    for k, (source, target) in enumerate(pairs):
        rows = source.shape[0] // STEPS
        part = pl.ds(pl.multiple_of(c * rows, rows), rows)
        copies.append(pltpu.make_async_copy(source.at[part], target.at[part], sems.at[k, c]))
    return copies


def start_chunks(pairs, sems):
    @pl.loop(0, STEPS)
    def _(c):
        for copy in chunk_copies(pairs, sems, c):
            copy.start()


def accumulate(total, left, right_ref):
    for c in range(0, WIDTH, COLUMNS):
        cols = slice(c, c + COLUMNS)
        total[cols] += dot_tn(right_ref[..., cols].reshape(left.shape[0], COLUMNS), left)


def experts_forward_kernel(
    x_hbm, mixed_hbm, gain_hbm, router_hbm, chosen_hbm, place_hbm, wattn_hbm, win_hbm, wout_hbm,
    y_ref, f_ref, scale_ref, logit_ref, gate_ref, middle_hbm, normed_hbm, g_hbm, u_hbm,
    x_ref, mixed_ref, gain_ref, router_ref, chosen_ref, place_ref, middle_ref, normed_ref,
    gate_rows, wattn, win, wout, g_all, u_all, total, small_sems, attn_sems, in_sems, out_sems,
):
    height = WIDTH // ATTN_CHUNKS
    mixed_copy, x_copy = copied(((mixed_hbm, mixed_ref), (x_hbm, x_ref)), small_sems)
    attn = [
        pltpu.make_async_copy(
            wattn_hbm.at[pl.ds(c * height, height)], wattn.at[pl.ds(c * height, height)], attn_sems.at[c]
        )
        for c in range(ATTN_CHUNKS)
    ]
    for copy in attn:
        copy.start()
    small = copied(
        (
            (gain_hbm, gain_ref),
            (router_hbm, router_ref),
            (chosen_hbm, chosen_ref),
            (place_hbm, place_ref),
        ),
        small_sems.at[pl.ds(2, 4)],
    )
    weights = ((win_hbm, win), (wout_hbm, wout))
    start_chunks(weights, in_sems)
    total[...] = jnp.zeros_like(total)
    mixed_copy.wait()
    x_copy.wait()

    squares = jnp.zeros((1, TOKENS), F32)
    for c in range(ATTN_CHUNKS):
        part = pl.ds(c * height, height)
        attn[c].wait()
        middle = x_ref[part].astype(F32) + dot_nn(wattn[part], mixed_ref[...])
        middle_ref[part] = middle
        squares += jnp.sum(middle * middle, axis=0, keepdims=True)
    scale = lax.rsqrt(squares * (1.0 / WIDTH) + EPSILON)
    scale_ref[...] = scale
    for copy in small:
        copy.wait()
    normed_ref[...] = (middle_ref[...] * scale * gain_ref[...]).astype(BF16)
    logits = dot_tn(router_ref[...], normed_ref[...])
    logit_ref[...] = logits
    chosen = chosen_ref[...] > 0.5
    top = jnp.max(jnp.where(chosen, logits, -1e30), axis=0, keepdims=True)
    raised = jnp.where(chosen, jnp.exp(jnp.where(chosen, logits - top, 0.0)), 0.0)
    gates = raised / jnp.sum(raised, axis=0, keepdims=True)
    gate_ref[...] = gates
    for e in range(EXPERTS):
        gate_rows[e] = gates[e : e + 1]

    leaving = copied(
        ((middle_ref, middle_hbm), (normed_ref, normed_hbm)), small_sems.at[pl.ds(6, 2)]
    )
    lane = lax.broadcasted_iota(jnp.int32, (SLOTS, 2 * HIDDEN), 1)
    hidden = ((g_all, g_hbm), (u_all, u_hbm))

    @pl.loop(0, STEPS)
    def _(c):
        some = pl.ds(c * BATCH, BATCH)
        rows = pl.ds(pl.multiple_of(c * BLOCK, BLOCK), BLOCK)
        win_copy, wout_copy = chunk_copies(weights, in_sems, c)
        win_copy.wait()
        g = dot_nn(win[some, 0].reshape(BLOCK, WIDTH), normed_ref[...])
        u = dot_nn(win[some, 1].reshape(BLOCK, WIDTH), normed_ref[...])
        g_all[rows] = g.astype(BF16)
        u_all[rows] = u.astype(BF16)
        for copy in chunk_copies(hidden, out_sems, c):
            copy.start()
        active = (g * jax.nn.sigmoid(g) * u).astype(BF16).astype(F32)
        gated = (active.reshape(BATCH, HIDDEN, TOKENS) * gate_rows[some]).astype(BF16)
        gated = gated.reshape(BLOCK, TOKENS)
        for q in range(0, BATCH, QUAD):
            pick = one_hot_slots(place_ref[pl.ds(c * BATCH + q, QUAD)])
            every = dot_nt(pick, gated[q * HIDDEN : (q + QUAD) * HIDDEN])
            for p in range(QUAD // 2):
                lanes = slice(2 * p * HIDDEN, 2 * (p + 1) * HIDDEN)
                even = every[2 * p * SLOTS : (2 * p + 1) * SLOTS, lanes]
                odd = every[(2 * p + 1) * SLOTS : (2 * p + 2) * SLOTS, lanes]
                row = pl.multiple_of((c * BATCH + q) // 2 * SLOTS + p * SLOTS, SLOTS)
                f_ref[pl.ds(row, SLOTS)] = jnp.where(lane < HIDDEN, even, odd).astype(BF16)
        wout_copy.wait()
        accumulate(total, gated, wout.at[some])

    y_ref[...] = total[...].astype(BF16)
    for copy in leaving:
        copy.wait()

    @pl.loop(0, STEPS)
    def _(c):
        for copy in chunk_copies(hidden, out_sems, c):
            copy.wait()


def vmem_spec():
    return pl.BlockSpec(memory_space=pltpu.VMEM)


def any_spec():
    return pl.BlockSpec(memory_space=pl.ANY)


def expert_scratch():
    return [
        pltpu.VMEM((EXPERTS, 2, HIDDEN, WIDTH), BF16),
        pltpu.VMEM((EXPERTS, HIDDEN, WIDTH), BF16),
        pltpu.VMEM((EXPERTS * HIDDEN, TOKENS), BF16),
        pltpu.VMEM((EXPERTS * HIDDEN, TOKENS), BF16),
        pltpu.VMEM((WIDTH, TOKENS), F32),
    ]


def expert_cost():
    return pl.CostEstimate(
        flops=6 * TOKENS * EXPERTS * HIDDEN * WIDTH, bytes_accessed=28_000_000, transcendentals=0
    )


def experts_forward(x, mixed, gain, router, chosen, places, w_attn, w_in, w_out):
    hidden = jax.ShapeDtypeStruct((EXPERTS * HIDDEN, TOKENS), BF16)
    some = jax.ShapeDtypeStruct((EXPERTS, TOKENS), F32)
    return pl.pallas_call(
        experts_forward_kernel,
        in_specs=[any_spec()] * 9,
        out_specs=[vmem_spec()] * 5 + [any_spec()] * 4,
        out_shape=[
            jax.ShapeDtypeStruct((WIDTH, TOKENS), BF16),
            jax.ShapeDtypeStruct((EXPERTS // 2 * SLOTS, 2 * HIDDEN), BF16),
            jax.ShapeDtypeStruct((1, TOKENS), F32),
            some,
            some,
            jax.ShapeDtypeStruct((WIDTH, TOKENS), F32),
            jax.ShapeDtypeStruct((WIDTH, TOKENS), BF16),
            hidden,
            hidden,
        ],
        scratch_shapes=[
            pltpu.VMEM((WIDTH, TOKENS), BF16),
            pltpu.VMEM((WIDTH, TOKENS), BF16),
            pltpu.VMEM((WIDTH, 1), F32),
            pltpu.VMEM((WIDTH, EXPERTS), BF16),
            pltpu.VMEM((EXPERTS, TOKENS), F32),
            pltpu.VMEM((EXPERTS, 1, TOKENS), F32),
            pltpu.VMEM((WIDTH, TOKENS), F32),
            pltpu.VMEM((WIDTH, TOKENS), BF16),
            pltpu.VMEM((EXPERTS, 1, TOKENS), F32),
            pltpu.VMEM((WIDTH, WIDTH), BF16),
        ]
        + expert_scratch()
        + [pltpu.SemaphoreType.DMA((8,)), pltpu.SemaphoreType.DMA((ATTN_CHUNKS,))]
        + [pltpu.SemaphoreType.DMA((2, STEPS))] * 2,
        compiler_params=pltpu.CompilerParams(vmem_limit_bytes=EXPERT_VMEM),
        cost_estimate=expert_cost(),
        name="experts_forward",
    )(x, mixed, gain, router, chosen, places, w_attn, w_in, w_out)


def experts_backward_kernel(
    dz_hbm, gain_hbm, gate_hbm, place_hbm, route_hbm,
    g_hbm, u_hbm, middle_hbm, win_hbm, wout_hbm,
    out_ref, du_ref,
    dz_ref, gain_ref, gate_ref, place_ref, route_ref,
    win, wout, g_all, u_all, total, middle_all, dgate_all, in_sems, small_sems,
):
    dz_copy, gate_copy, place_copy = copied(
        ((dz_hbm, dz_ref), (gate_hbm, gate_ref), (place_hbm, place_ref)), small_sems
    )
    pairs = ((wout_hbm, wout), (g_hbm, g_all), (u_hbm, u_all), (win_hbm, win))
    start_chunks(pairs, in_sems)
    total[...] = jnp.zeros_like(total)
    late = copied(
        ((middle_hbm, middle_all), (gain_hbm, gain_ref), (route_hbm, route_ref)),
        small_sems.at[pl.ds(3, 3)],
    )
    dz_copy.wait()
    gate_copy.wait()
    place_copy.wait()

    @pl.loop(0, STEPS)
    def _(c):
        some = pl.ds(c * BATCH, BATCH)
        rows = pl.ds(pl.multiple_of(c * BLOCK, BLOCK), BLOCK)
        wout_copy, g_copy, u_copy, win_copy = chunk_copies(pairs, in_sems, c)
        wout_copy.wait()
        through = dot_nn(wout[some].reshape(BLOCK, WIDTH), dz_ref[...])
        g_copy.wait()
        u_copy.wait()
        g = g_all[rows].astype(F32)
        u = u_all[rows].astype(F32)
        sig = jax.nn.sigmoid(g)
        silu = g * sig
        active = (silu * u).astype(BF16).astype(F32)
        dgate_all[pl.ds(pl.multiple_of(c * BATCH, BATCH), BATCH)] = jnp.sum(
            (active * through).reshape(BATCH, HIDDEN, TOKENS), axis=1
        )
        df = (through.reshape(BATCH, HIDDEN, TOKENS) * gate_ref[some]).reshape(BLOCK, TOKENS)
        dg = (df * u * (sig * (1.0 + g * (1.0 - sig)))).astype(BF16)
        du = (df * silu).astype(BF16)
        both = jnp.concatenate(
            [dg.reshape(BATCH, 1, HIDDEN, TOKENS), du.reshape(BATCH, 1, HIDDEN, TOKENS)], axis=1
        ).reshape(2 * BLOCK, TOKENS)
        for q in range(0, BATCH, QUAD):
            pick = one_hot_slots(place_ref[pl.ds(c * BATCH + q, QUAD)])
            every = dot_nt(pick, both[2 * q * HIDDEN : 2 * (q + QUAD) * HIDDEN])
            for e in range(QUAD):
                row = pl.multiple_of((c * BATCH + q + e) * SLOTS, SLOTS)
                du_ref[pl.ds(row, SLOTS)] = every[
                    e * SLOTS : (e + 1) * SLOTS, 2 * e * HIDDEN : 2 * (e + 1) * HIDDEN
                ].astype(BF16)
        win_copy.wait()
        accumulate(total, both, win.at[some])

    for copy in late:
        copy.wait()
    inner = jnp.zeros((1, TOKENS), F32)
    for w in range(N_WA):
        part = pl.ds(w * OWN, OWN)
        share = total[part].astype(BF16)
        out_ref[w, :OWN] = share
        inner += jnp.sum(
            share.astype(F32) * middle_all[part] * gain_ref[part], axis=0, keepdims=True
        )
    expert = lax.broadcasted_iota(jnp.int32, (EXPERTS, TOKENS), 0)
    dgate = dgate_all[...]
    tops = [
        jnp.sum(jnp.where(expert == route_ref[k : k + 1], dgate, 0.0), axis=0, keepdims=True)
        for k in range(TOP)
    ]
    high = inner.astype(BF16).astype(F32)
    extra = jnp.concatenate(
        tops + [high, inner - high, jnp.zeros((EXTRA - TOP - 2, TOKENS), F32)], axis=0
    ).astype(BF16)
    for w in range(N_WA):
        out_ref[w, OWN:] = extra


def experts_backward(dz, gain, gates, places, routes, g, u, middle, w_in, w_out):
    return pl.pallas_call(
        experts_backward_kernel,
        in_specs=[any_spec()] * 10,
        out_specs=[vmem_spec()] * 2,
        out_shape=[
            jax.ShapeDtypeStruct((N_WA, OWN + EXTRA, TOKENS), BF16),
            jax.ShapeDtypeStruct((EXPERTS * SLOTS, 2 * HIDDEN), BF16),
        ],
        scratch_shapes=[
            pltpu.VMEM((WIDTH, TOKENS), BF16),
            pltpu.VMEM((WIDTH, 1), F32),
            pltpu.VMEM((EXPERTS, 1, TOKENS), F32),
            pltpu.VMEM((EXPERTS, 1, TOKENS), F32),
            pltpu.VMEM((TOP, TOKENS), jnp.int32),
        ]
        + expert_scratch()
        + [
            pltpu.VMEM((WIDTH, TOKENS), F32),
            pltpu.VMEM((EXPERTS, TOKENS), F32),
            pltpu.SemaphoreType.DMA((4, STEPS)),
            pltpu.SemaphoreType.DMA((6,)),
        ],
        compiler_params=pltpu.CompilerParams(vmem_limit_bytes=EXPERT_VMEM),
        cost_estimate=expert_cost(),
        name="experts_backward",
    )(dz, gain, gates, places, routes, g, u, middle, w_in, w_out)


def slot_rows(feature_ref, place_ref):
    rows = []
    for s in range(N_SEQ):
        rows.append(dot_nt(one_hot_slots(place_ref[s]), feature_ref[s]).astype(BF16))
    return [
        jnp.concatenate([r[e * SLOTS : (e + 1) * SLOTS] for r in rows], axis=0)
        for e in range(QUAD)
    ]


def weight_grad_in_kernel(compact_ref, feature_ref, place_ref, out_ref):
    rows = slot_rows(feature_ref, place_ref)
    for e in range(QUAD):
        left = jnp.concatenate(
            [compact_ref[s, e * SLOTS : (e + 1) * SLOTS] for s in range(N_SEQ)], axis=0
        )
        out_ref[e] = dot_tn(left, rows[e])


def weight_grad_out_kernel(compact_ref, feature_ref, place_ref, out_ref):
    rows = slot_rows(feature_ref, place_ref)
    for p in range(QUAD // 2):
        left = jnp.concatenate(
            [compact_ref[s, p * SLOTS : (p + 1) * SLOTS] for s in range(N_SEQ)], axis=0
        )
        out_ref[2 * p] = dot_tn(left, rows[2 * p])[:HIDDEN]
        out_ref[2 * p + 1] = dot_tn(left, rows[2 * p + 1])[HIDDEN:]


def weight_grad(kernel, compact, feature, places, height):
    block = compact.shape[1] * QUAD // EXPERTS
    return pl.pallas_call(
        kernel,
        grid=(EXPERTS // QUAD,),
        in_specs=[
            pl.BlockSpec((N_SEQ, block, 2 * HIDDEN), lambda i: (0, i, 0)),
            pl.BlockSpec((N_SEQ, OWN, TOKENS), lambda i: (0, 0, 0)),
            pl.BlockSpec((N_SEQ, QUAD, 1, TOKENS), lambda i: (0, i, 0, 0)),
        ],
        out_specs=pl.BlockSpec((QUAD, height, OWN), lambda i: (i, 0, 0)),
        out_shape=jax.ShapeDtypeStruct((EXPERTS, height, OWN), F32),
        compiler_params=params(),
        cost_estimate=pl.CostEstimate(
            flops=2 * N_SEQ * TOKENS * EXPERTS * SLOTS * OWN, bytes_accessed=15_000_000, transcendentals=0
        ),
        name="expert_weight_grad",
    )(compact, feature, places)


def weight_grad_in(compact, feature, places):
    return weight_grad(weight_grad_in_kernel, compact, feature, places, 2 * HIDDEN)


def weight_grad_out(compact, feature, places):
    return weight_grad(weight_grad_out_kernel, compact, feature, places, HIDDEN)


def causal_mask(first):
    key = lax.broadcasted_iota(jnp.int32, (LENGTH, ROWS), 0)
    query = lax.broadcasted_iota(jnp.int32, (LENGTH, ROWS), 1) + first
    return key <= query


def side_by_side(parts):
    return jnp.concatenate(parts, axis=1)


def attention_forward_kernel(first_ref, q_ref, kv_ref, o_ref, lse_ref):
    keys = side_by_side([kv_ref[s, :HEAD_DIM] for s in range(N_SEQ)])
    values = side_by_side([kv_ref[s, HEAD_DIM:] for s in range(N_SEQ)])
    keep = causal_mask(first_ref[0])
    for h in range(PER_GROUP):
        rows = slice(h * HEAD_DIM, (h + 1) * HEAD_DIM)
        scores = jnp.where(keep, dot_tn(keys, q_ref[rows]) * SCALE, -1e30)
        top = jnp.max(scores, axis=0, keepdims=True)
        raised = jnp.exp(scores - top)
        total = jnp.sum(raised, axis=0, keepdims=True)
        probs = (raised * (1.0 / total)).astype(BF16)
        o_ref[rows] = dot_nn(values, probs).astype(BF16)
        lse_ref[h] = top + jnp.log(total)


def attention_forward(first, q, kv):
    return pl.pallas_call(
        attention_forward_kernel,
        grid=(MICRO,),
        in_specs=[
            pl.BlockSpec(memory_space=pltpu.SMEM),
            pl.BlockSpec((PER_GROUP * HEAD_DIM, ROWS), lambda m: (0, m)),
            pl.BlockSpec((N_SEQ, 2 * HEAD_DIM, ROWS), lambda m: (0, 0, m)),
        ],
        out_specs=[
            pl.BlockSpec((PER_GROUP * HEAD_DIM, ROWS), lambda m: (0, m)),
            pl.BlockSpec((PER_GROUP, 1, ROWS), lambda m: (0, 0, m)),
        ],
        out_shape=[
            jax.ShapeDtypeStruct((PER_GROUP * HEAD_DIM, TOKENS), BF16),
            jax.ShapeDtypeStruct((PER_GROUP, 1, TOKENS), F32),
        ],
        compiler_params=params(),
        name="attention_forward",
    )(first, q, kv)


def attention_backward_kernel(first_ref, q_ref, kv_ref, o_ref, do_ref, lse_ref, dq_ref, dkv_ref):
    keys = side_by_side([kv_ref[s, :HEAD_DIM] for s in range(N_SEQ)])
    values = side_by_side([kv_ref[s, HEAD_DIM:] for s in range(N_SEQ)])
    keep = causal_mask(first_ref[0])
    dkeys = jnp.zeros((HEAD_DIM, LENGTH), F32)
    dvalues = jnp.zeros((HEAD_DIM, LENGTH), F32)
    for h in range(PER_GROUP):
        rows = slice(h * HEAD_DIM, (h + 1) * HEAD_DIM)
        query = q_ref[rows]
        dout = do_ref[rows]
        scores = jnp.where(keep, dot_tn(keys, query) * SCALE, -1e30)
        probs = jnp.exp(scores - lse_ref[h])
        dvalues += dot_nt(dout, probs.astype(BF16))
        inner = jnp.sum(
            dout.astype(F32) * o_ref[rows].astype(F32), axis=0, keepdims=True
        )
        dscores = (probs * (dot_tn(values, dout) - inner)).astype(BF16)
        dkeys += dot_nt(query, dscores)
        dq_ref[rows] = dot_nn(keys, dscores) * SCALE
    dkeys = (dkeys * SCALE).astype(BF16)
    dvalues = dvalues.astype(BF16)
    for s in range(N_SEQ):
        lanes = slice(s * ROWS, (s + 1) * ROWS)
        dkv_ref[s, :HEAD_DIM] = dkeys[:, lanes]
        dkv_ref[s, HEAD_DIM:] = dvalues[:, lanes]


def attention_backward(first, q, kv, o, do, lse):
    q_spec = pl.BlockSpec((PER_GROUP * HEAD_DIM, ROWS), lambda m: (0, m))
    kv_spec = pl.BlockSpec((N_SEQ, 2 * HEAD_DIM, ROWS), lambda m: (0, 0, m))
    return pl.pallas_call(
        attention_backward_kernel,
        grid=(MICRO,),
        in_specs=[
            pl.BlockSpec(memory_space=pltpu.SMEM),
            q_spec,
            kv_spec,
            q_spec,
            q_spec,
            pl.BlockSpec((PER_GROUP, 1, ROWS), lambda m: (0, 0, m)),
        ],
        out_specs=[q_spec, kv_spec],
        out_shape=[
            jax.ShapeDtypeStruct((PER_GROUP * HEAD_DIM, TOKENS), F32),
            jax.ShapeDtypeStruct((N_SEQ, 2 * HEAD_DIM, TOKENS), BF16),
        ],
        compiler_params=params(),
        name="attention_backward",
    )(first, q, kv, o, do, lse)


def rotate(values, cosine, sine):
    half = HEAD_DIM // 2
    a, b = values[:, :half], values[:, half:]
    return jnp.concatenate([a * cosine - b * sine, b * cosine + a * sine], axis=1)


def high_low(values):
    high = lax.reduce_precision(values, 8, 7)
    return high.astype(BF16), (values - high).astype(BF16)


def after(value, *others):
    return lax.optimization_barrier((value,) + others)[0]


def exchange(blocks, axis):
    return lax.all_to_all(blocks, axis, split_axis=0, concat_axis=0, tiled=False)


def summed(blocks, axis):
    return jnp.sum(exchange(blocks, axis).astype(F32), axis=0)


def on_device(
    first_layer_input,
    routes,
    cotangent,
    gains,
    qkv_weight,
    out_weight,
    router_weight,
    expert_in,
    expert_out,
):
    section_first = lax.axis_index("section") == 0
    s_index = lax.axis_index("seq")
    w_index = lax.axis_index("wa")
    first = jnp.reshape(s_index * ROWS, (1,)).astype(jnp.int32)

    def rows_of(values):
        return lax.all_gather(values, "wa", axis=0, tiled=True)

    def own(values):
        return lax.dynamic_slice_in_dim(values, w_index * OWN, OWN, 0)

    def lanes(values):
        return jnp.concatenate([values[0], values[1]], axis=1)

    def reduced(blocks):
        pairs = blocks.reshape((chips, 2) + blocks.shape[1:])
        kept = lax.dynamic_index_in_dim(pairs, core, 1, False).astype(F32)
        sent = lax.dynamic_index_in_dim(pairs, 1 - core, 1, False)
        kept += lax.ppermute(sent, "wa", [(i, i ^ 1) for i in range(N_WA)]).astype(F32)
        total = lax.dynamic_index_in_dim(kept, chip, 0, False)
        kept = kept.astype(BF16)
        for d in (1, chips - 1, 2):
            route = [(i, (i // 2 + d) % chips * 2 + i % 2) for i in range(N_WA)]
            sent = lax.dynamic_index_in_dim(kept, (chip + d) % chips, 0, False)
            total += lax.ppermute(sent, "wa", route).astype(F32)
        return total

    core, chip, chips = w_index % 2, w_index // 2, N_WA // 2

    def gathered(block):
        arrived = []
        for d in (chips - 1, 2, 1):
            route = [(i, (i // 2 + d) % chips * 2 + i % 2) for i in range(N_WA)]
            arrived.append(lax.ppermute(block, "wa", route))
        mine = jnp.concatenate(arrived + [block], axis=0)
        return mine, lax.ppermute(mine, "wa", [(i, i ^ 1) for i in range(N_WA)])

    def to_arrival(columns):
        parts = columns.reshape(columns.shape[0], chips, 2, -1)
        parts = lax.dynamic_slice_in_dim(
            jnp.concatenate([parts, parts], axis=1), chip + 1, chips, 1
        )
        return lax.optimization_barrier(
            tuple(
                lax.dynamic_index_in_dim(parts, c, 2, False).reshape(columns.shape[0], -1)
                for c in (core, 1 - core)
            )
        )

    def from_arrival(halves):
        mine, other = (
            lax.dynamic_slice_in_dim(
                jnp.concatenate([half.reshape(half.shape[0], chips, -1)] * 2, axis=1),
                chips - 1 - chip,
                chips,
                1,
            )
            for half in halves
        )
        pairs = [jnp.where(core == 0, mine, other), jnp.where(core == 0, other, mine)]
        return jnp.stack(pairs, axis=2).reshape(mine.shape[0], -1)

    def of_section(one, two):
        return jnp.where(section_first, one, two)

    x_first = lanes(first_layer_input)
    cot = lanes(cotangent)
    gain_pair = gains[0].T
    gain_high = lax.reduce_precision(gain_pair, 8, 7)
    gain_rest, gain_low = high_low(gain_pair - gain_high)
    gain_high = gain_high.astype(BF16)
    w_qkv = qkv_weight[0]
    w_qkv_blocks = jnp.transpose(w_qkv.reshape(OWN, KV_HEADS, GROUP_COLS), (1, 0, 2))
    packed = jnp.concatenate([x_first, router_weight[0], gain_high, gain_rest, gain_low], axis=1)
    packed, w_qkv_blocks = lax.optimization_barrier((packed, w_qkv_blocks))
    w_qkv_group = exchange(w_qkv_blocks, "wa").reshape(WIDTH, GROUP_COLS)
    packed = rows_of(packed)
    x_first_full = packed[:, :TOKENS]
    w_router = packed[:, TOKENS : TOKENS + EXPERTS]
    gain_parts = packed[:, TOKENS + EXPERTS :].astype(F32)
    gain_parts = gain_parts[:, 0:2] + gain_parts[:, 2:4] + gain_parts[:, 4:6]
    gain_one, gain_two = gain_parts[:, 0:1], gain_parts[:, 1:2]
    w_qkv_wide = to_arrival(
        jnp.pad(
            w_qkv.reshape(OWN, KV_HEADS, GROUP_COLS),
            ((0, 0), (0, 0), (0, SENT_COLS - GROUP_COLS)),
        ).reshape(OWN, KV_HEADS * SENT_COLS)
    )
    w_attn_full = rows_of(after(out_weight[0], packed, w_qkv_group))
    w_attn_group = to_arrival(lax.dynamic_slice_in_dim(w_attn_full, w_index * OWN, OWN, 1).T)
    cot_full = rows_of(cot)
    w_in = expert_in[0]
    w_out = expert_out[0]
    own_gain_one = gains[0, 0][:, None]
    own_gain_two = gains[0, 1][:, None]

    position = (s_index * ROWS + jnp.arange(ROWS, dtype=jnp.int32)).astype(F32)
    frequency = 10000.0 ** (
        -jnp.arange(HEAD_DIM // 2).astype(F32) * (2.0 / HEAD_DIM)
    )
    angle = frequency[:, None] * position[None, :]
    cosine = jnp.tile(jnp.cos(angle), (1, MICRO))
    sine = jnp.tile(jnp.sin(angle), (1, MICRO))

    experts = jnp.arange(EXPERTS, dtype=jnp.int32)[None, :, None]
    chosen = jnp.zeros((MICRO, EXPERTS, ROWS), F32)
    for k in range(TOP):
        chosen += (routes[0][:, None, :, k] == experts).astype(F32)
    earlier = jnp.triu(jnp.ones((ROWS, ROWS), BF16), 1)
    rank = jnp.einsum("met,tu->meu", chosen.astype(BF16), earlier, preferred_element_type=F32)
    micro = jnp.arange(MICRO, dtype=jnp.int32).astype(F32)[:, None, None]
    place = lanes(jnp.where(chosen > 0.5, rank + CAP * micro, -1.0))
    chosen = lanes(chosen)
    places = place[:, None, :]
    route_lanes = jnp.concatenate([routes[0, 0].T, routes[0, 1].T], axis=1)
    picked = (
        route_lanes[:, None, :] == jnp.arange(EXPERTS, dtype=jnp.int32)[None, :, None]
    )

    def norm_scale(values):
        return lax.rsqrt(jnp.mean(values * values, axis=0, keepdims=True) + EPSILON)

    def for_seq(parts, shared):
        blocks = jnp.concatenate(
            [
                jnp.transpose(part.astype(BF16).reshape(OWN, N_SEQ, -1), (1, 0, 2))
                for part in parts
            ],
            axis=2,
        )
        shared = jnp.concatenate(high_low(shared), axis=1)
        return jnp.concatenate(
            [blocks, jnp.broadcast_to(shared[None], (N_SEQ,) + shared.shape)], axis=2
        )

    def from_seq(blocks, n):
        total = jnp.sum(blocks.astype(F32), axis=0)
        k = (total.shape[1] - n) // 2
        return total[:, :n], total[:, n : n + k] + total[:, n + k :]

    def forward(x_own, x_full):
        x = x_full.astype(F32)
        scale_one = norm_scale(x)
        normed_one = (x * scale_one * gain_one).astype(BF16)
        heads = dot_tn(w_qkv_group, normed_one).reshape(PER_GROUP + 2, HEAD_DIM, TOKENS)
        turned = rotate(heads[: PER_GROUP + 1], cosine, sine)
        turned = jnp.concatenate([turned, heads[PER_GROUP + 1 :]], axis=0).astype(BF16)
        turned = turned.reshape(GROUP_COLS, TOKENS)
        queries = turned[: PER_GROUP * HEAD_DIM]
        sent = turned[PER_GROUP * HEAD_DIM :]
        key_value = exchange(jnp.broadcast_to(sent[None], (N_SEQ,) + sent.shape), "seq")
        mixed, log_total = attention_forward(first, queries, key_value)
        mixed_full = rows_of(mixed)
        part, compact, scale_two, logits, gates, middle, normed_two, g, u = experts_forward(
            x_full, mixed_full, gain_two, w_router, chosen, places, w_attn_full, w_in, w_out
        )
        saved = (
            x_own,
            scale_one,
            own(normed_one),
            queries,
            key_value,
            log_total,
            mixed,
            mixed_full,
            middle,
            scale_two,
            normed_two,
            logits,
            gates,
            g,
            u,
        )
        return part.reshape(N_WA, OWN, TOKENS), compact, saved

    def finish(saved, total):
        return (own(saved[8]) + total).astype(BF16)

    def backward(dz, dz_full, saved, alongside, feature, later):
        (
            x_own,
            scale_one,
            own_normed_one,
            queries,
            key_value,
            log_total,
            mixed,
            mixed_full,
            middle,
            scale_two,
            normed_two,
            logits,
            gates,
            g,
            u,
        ) = saved
        blocks, du = experts_backward(
            dz_full, gain_two, gates[:, None, :], places, route_lanes, g, u, middle, w_in, w_out
        )
        blocks, alongside = lax.optimization_barrier((blocks, alongside))
        back = reduced(blocks)
        if later is not None:
            du = of_section(du, later[0])
            back, du = lax.optimization_barrier((back, du))
        dgate_top = back[OWN : OWN + TOP]
        inner = back[OWN + TOP : OWN + TOP + 1] + back[OWN + TOP + 1 : OWN + TOP + 2]
        dgate = jnp.sum(jnp.where(picked, dgate_top[:, None, :], 0.0), axis=0)
        dlogit = gates * (dgate - jnp.sum(gates * dgate, axis=0, keepdims=True))
        dlogit_low = dlogit.astype(BF16)
        dnormed = back[:OWN] + dot_nn(router_weight[0], dlogit_low)
        inner += jnp.sum(dlogit * logits, axis=0, keepdims=True) / scale_two
        own_middle = own(middle)
        dmiddle = (
            dz.astype(F32)
            + scale_two * own_gain_two * dnormed
            - own_middle * (scale_two * scale_two * scale_two * inner * (1.0 / WIDTH))
        )
        gain_two_grad = jnp.sum(dnormed * own_middle * scale_two, axis=1, keepdims=True)
        own_normed_two = own(normed_two)
        router_grad = dot_nt(own_normed_two, dlogit_low)
        dmiddle_low = dmiddle.astype(BF16)
        attn_grad = dot_nt(dmiddle_low, mixed_full)
        small_grad = jnp.concatenate([gain_two_grad, router_grad], axis=1)
        dmiddle_full = gathered(dmiddle_low)
        dmixed = sum(dot_nn(w, d) for w, d in zip(w_attn_group, dmiddle_full)).astype(BF16)
        dq, dkv = attention_backward(first, queries, key_value, mixed, dmixed, log_total)
        dkv = summed(dkv, "seq")
        dturned = jnp.concatenate([dq, dkv], axis=0)
        turned = jnp.concatenate(
            [queries, lax.dynamic_index_in_dim(key_value, s_index, 0, False)], axis=0
        )
        inner_one = jnp.sum(dturned * turned.astype(F32), axis=0, keepdims=True)
        dheads = dturned.reshape(PER_GROUP + 2, HEAD_DIM, TOKENS)
        dheads = jnp.concatenate(
            [rotate(dheads[: PER_GROUP + 1], cosine, -sine), dheads[PER_GROUP + 1 :]], axis=0
        )
        sent = jnp.concatenate(
            [
                dheads.reshape(GROUP_COLS, TOKENS).astype(BF16),
                *high_low(inner_one),
                jnp.zeros((14, TOKENS), BF16),
            ],
            axis=0,
        )
        full = gathered(sent)
        if later is not None:
            places_all = alongside[0][:, OWN : OWN + EXPERTS].astype(F32)[:, :, None, :]
            expert_out_grad = weight_grad_out(alongside[1], alongside[0], places_all)
            attn_grad, small_grad = jax.tree.map(of_section, (attn_grad, small_grad), later[1:3])
            blocks = jnp.concatenate([feature, for_seq((attn_grad,), small_grad)], axis=2)
            blocks = exchange(blocks, "seq")
            full, expert_out_grad, blocks = lax.optimization_barrier(
                (full, expert_out_grad, blocks)
            )
            feature = blocks
            attn_grad, small_grad = from_seq(blocks[:, :, TOKENS:], OWN)
        inner_one = jnp.sum(
            jnp.stack([half.reshape(chips, SENT_COLS, TOKENS) for half in full])[
                :, :, GROUP_COLS : GROUP_COLS + 2
            ].astype(F32),
            axis=(0, 1, 2),
        )[None] / scale_one
        dnormed_one = sum(dot_nn(w, d) for w, d in zip(w_qkv_wide, full))
        x = x_own.astype(F32)
        dx = (
            dmiddle
            + scale_one * own_gain_one * dnormed_one
            - x * (scale_one * scale_one * scale_one * inner_one * (1.0 / WIDTH))
        )
        gain_one_grad = jnp.sum(dnormed_one * x * scale_one, axis=1, keepdims=True)
        qkv_grad = tuple(dot_nt(own_normed_one, half).astype(BF16) for half in full)
        if later is None:
            return dx, alongside, (du, attn_grad, small_grad, gain_one_grad, qkv_grad)
        gain_one_grad, qkv_grad = jax.tree.map(of_section, (gain_one_grad, qkv_grad), later[3:])
        blocks = exchange(for_seq((from_arrival(qkv_grad),), gain_one_grad), "seq")
        expert_in_grad = weight_grad_in(
            lax.all_gather(du, "seq", axis=0, tiled=False), feature, places_all
        )
        blocks, expert_in_grad = lax.optimization_barrier((blocks, expert_in_grad))
        qkv_grad, gain_one_grad = from_seq(blocks, SENT_COLS)
        small_grad = jnp.concatenate([gain_one_grad, small_grad], axis=1)
        return dx, expert_in_grad, expert_out_grad, attn_grad, qkv_grad, small_grad

    out_one, compact_one, saved_one = forward(x_first, x_first_full)
    out_one = finish(saved_one, reduced(out_one))
    received = lax.ppermute(out_one, "section", [(0, 1)])
    out_two, compact_two, saved_two = forward(received, rows_of(received))
    out_two = exchange(out_two, "wa")

    feature_in = of_section(saved_one[10], saved_two[10]).reshape(N_SEQ, OWN, TOKENS)
    compact_out = lax.all_gather(of_section(compact_one, compact_two), "seq", axis=0, tiled=False)

    dx_two, out_two, later = backward(cot, cot_full, saved_two, out_two, None, None)
    out_two = finish(saved_two, jnp.sum(out_two.astype(F32), axis=0))
    returned = lax.ppermute(dx_two.astype(BF16), "section", [(1, 0)])
    returned_full = rows_of(returned)
    riders = jnp.concatenate([place, jnp.zeros((8, TOKENS), F32)], axis=0).astype(BF16)
    feature_out = jnp.concatenate(
        [
            of_section(returned_full, cot_full).reshape(N_SEQ, OWN, TOKENS),
            jnp.broadcast_to(riders[None], (N_SEQ,) + riders.shape),
        ],
        axis=1,
    )
    feature_out = exchange(feature_out, "seq")
    dx_one, expert_in_grad, expert_out_grad, attn_grad, qkv_grad, small_grad = backward(
        returned, returned_full, saved_one, (feature_out, compact_out), feature_in, later
    )

    def tokens_first(values):
        return jnp.transpose(values.reshape(OWN, MICRO, ROWS), (1, 2, 0))[None]

    return (
        tokens_first(of_section(out_one, out_two)),
        tokens_first(of_section(dx_one, dx_two)),
        small_grad[:, :2].T[None],
        qkv_grad[None, :, :GROUP_COLS],
        attn_grad[None],
        small_grad[None, :, 2:],
        expert_in_grad.reshape(1, EXPERTS, 2, HIDDEN, OWN),
        expert_out_grad[None],
    )


def solution(mesh):
    return jax.shard_map(
        on_device,
        mesh=mesh,
        in_specs=(
            P(None, "wa", "seq"),
            P("section", None, "seq", None),
            P(None, "wa", "seq"),
            P("section", None, "wa"),
            P("section", "wa", None),
            P("section", "wa", None),
            P("section", "wa", None),
            P("section", None, None, "wa", None),
            P("section", None, "wa", None),
        ),
        out_specs=(
            P("section", None, "seq", "wa"),
            P("section", None, "seq", "wa"),
            P("section", None, "wa"),
            P("section", "wa", "seq"),
            P("section", "wa", "seq"),
            P("section", "wa", None),
            P("section", None, None, "wa", "seq"),
            P("section", None, "wa", "seq"),
        ),
        check_vma=False,
    )
```
